768 devices in a mesh: rep: 12 (over z), bal: 8 (over y), tab: 8 (over x, core).
Axes of the slice: x: 4, y: 8, z: 12, core: 2. Of those that a mesh axis runs over, the one named last changes fastest.
Arguments:
- hot_rows: float32 [245760, 1024], P(('rep', 'bal', 'tab')), may hold values from -640 to 640
- cold_rows: bfloat16 [245760, 1024], P(('rep', 'bal', 'tab')), may hold values from -640 to 640
- row_source: int32 [294912, 1], P(('rep', 'bal', 'tab')), may hold values from 0 to 15; in each aligned block of 384 rows (0 to 383, 384 to 767, ...) at most 40 rows name the same one
- lengths: int32 [12, 8, 8, 8], P('rep', None, 'tab'), may hold values from 8 to 88, as said below
- destination: int32 [12, 8, 8, 8], P('rep', None, 'tab'), may hold values from 0 to 7, as said below
- proj_weight: bfloat16 [1024, 4096], replicated, may hold values from -0.1875 to 0.1875
- out_grad: bfloat16 [294912, 1024], P(('rep', 'bal', 'tab')), may hold values from -0.01171875 to 0.01171875
Outputs:
- attention_out: bfloat16 [294912, 1024], P(('rep', 'bal', 'tab'))
- grad_out_proj: bfloat16 [1024, 1024], P(('bal', 'tab'))
The draws below stay inside these ranges and needn't reach their ends.
Inputs may be any that keep to these rules, and one draw needn't show every extreme that they name: `row_source`: code shard + 8 * tier of each position's row (tier 0 float32, tier 1 bfloat16); among the positions of one device no code occurs more than 40 times. lengths[r, s, t, h] is the length of history h of device (r, s, t); each device's lengths sum to 384; the histories that the devices of one bal group send to any one of them also sum to 384; the devices of one bal group hold the same lengths in different orders, and each group has a history of exactly 88. destination[r, s, t, :] is a permutation of 0 to 7: every device sends one history to each device of its bal group.
All inputs are finite; a program needn't handle non-finite values.
Results may differ from the reference program's by a relative error of at most 0.02.
Values may be sent and summed in bfloat16 or wider, within the bound.
A program may use at most 64 MiB of HBM per device.

```python
import math
import jax
import jax.numpy as jnp
import numpy as np
from jax import lax

D = 1024
HEADS = 8
HEAD = 128
HOME_TOK = 384
MINLEN = 8
MAXLEN = 88
MOST = 40
TOKENS = 294912
N_REP = 12
N_BAL = 8
N_TAB = 8


def spread_rows(key, values, scale_top):
    key_row, key_col = jax.random.split(key)
    row_scale = jnp.exp(jax.random.uniform(key_row, (values.shape[0], 1), jnp.float32, 0.0, math.log(scale_top)))
    col_scale = jnp.exp(jax.random.uniform(key_col, (1, values.shape[1]), jnp.float32, 0.0, math.log(scale_top)))
    return values * row_scale * col_scale


def draw_hot_rows(key, part):
    key = jax.random.fold_in(key, 11)
    key_val, key_scale = jax.random.split(key)
    row_shape = (N_REP * N_BAL * N_TAB * N_TAB * MOST, D)
    values = jnp.clip(jax.random.normal(key_val, row_shape, jnp.float32), -6.0, 6.0)
    return spread_rows(key_scale, values, 10.0)


def draw_cold_rows(key, part):
    key = jax.random.fold_in(key, 12)
    key_val, key_scale = jax.random.split(key)
    row_shape = (N_REP * N_BAL * N_TAB * N_TAB * MOST, D)
    values = jnp.clip(jax.random.normal(key_val, row_shape, jnp.float32), -6.0, 6.0)
    return spread_rows(key_scale, values, 10.0).astype(jnp.bfloat16)


def regroup(table):
    return table.reshape(N_REP, N_TAB, N_BAL, N_BAL).transpose(0, 2, 1, 3)


def group_plan(key):
    group_count = N_REP * N_TAB
    pair_count = N_BAL // 2
    mean_len = HOME_TOK // N_BAL
    key_len, key_shift, key_dest = jax.random.split(key, 3)
    first_len = jax.random.randint(key_len, (group_count, pair_count), MINLEN, MAXLEN + 1)
    first_len = first_len.at[:, 0].set(MAXLEN)
    base_len = jnp.stack([first_len, 2 * mean_len - first_len], axis=2).reshape(group_count, N_BAL)
    member_ids = jnp.arange(N_BAL, dtype=jnp.int32)
    shift_scores = jax.random.randint(key_shift, (group_count, N_BAL), 0, 1 << 20) * N_BAL + member_ids
    shift_perm = jnp.argsort(shift_scores, axis=1).astype(jnp.int32)
    dest_scores = jax.random.randint(key_dest, (group_count, N_BAL, N_BAL), 0, 1 << 20) * N_BAL + member_ids
    dest_perm = jnp.argsort(dest_scores, axis=2).astype(jnp.int32)
    base_index = (shift_perm[:, :, None] + dest_perm) % N_BAL
    spread_base = jnp.broadcast_to(base_len[:, None, :], (group_count, N_BAL, N_BAL))
    history_len = jnp.take_along_axis(spread_base, base_index, axis=2)
    return (regroup(history_len).astype(jnp.int32), regroup(dest_perm).astype(jnp.int32))


def draw_lengths(key, part):
    history_len, dest_perm = group_plan(key)
    return history_len


def draw_destination(key, part):
    history_len, dest_perm = group_plan(key)
    return dest_perm


def level_of(stream_key, extent, shards, smallest, largest):
    loudness = 1.0
    for position, parts in shards:
        draws = jax.random.uniform(jax.random.fold_in(jax.random.fold_in(stream_key, 6), position), (parts,), jnp.float32, smallest / len(shards), largest / len(shards))
        loudness = loudness * jnp.repeat(jnp.exp(draws), extent[position] // parts).reshape((-1,) + (1,) * (len(extent) - 1 - position))
    return loudness


def shared_out(key, own, number, rows, amount, top, limit, slope):
    ranking = jax.random.permutation(key, amount)
    crowded, common = shares(amount, rows * top, limit, slope, True), shares(amount, rows * top, limit, slope, False)
    places = jnp.arange(amount)

    def named(tallies, rotation):
        used = int((tallies > 0).sum())
        fixed = max(1, used // 4)
        passed = fixed + (places - fixed + rotation * (used - fixed)) % max(1, amount - fixed)
        return jnp.zeros((amount,), jnp.int32).at[ranking[jnp.where(places < fixed, places, passed)]].set(jnp.asarray(tallies, jnp.int32))

    tallies = jnp.where(number % 4 == 0, named(crowded, number // 4), named(common, number - number // 4 - 1))
    mixed = jax.random.permutation(jax.random.fold_in(own, 3), amount)
    donor, receiver = mixed[0:amount // 2 * 2:2], mixed[1:amount // 2 * 2:2]
    slack = jnp.minimum(tallies[donor] - 1, limit - tallies[receiver]) // 2
    slack = jnp.where((donor == ranking[0]) | (receiver == ranking[0]) | (tallies[receiver] == 0), 0, jnp.maximum(slack, 0))
    passed = jax.random.randint(jax.random.fold_in(own, 4), (amount // 2,), 0, 1 << 20) % (slack + 1)
    tallies = tallies.at[donor].add(-passed).at[receiver].add(passed)
    labels = jnp.searchsorted(jnp.cumsum(tallies), jnp.arange(rows * top), side="right").astype(jnp.int32)
    listing = labels.reshape(top, rows).T
    listing = listing[jax.random.permutation(jax.random.fold_in(own, 1), rows)]
    rotation = jax.random.randint(jax.random.fold_in(own, 2), (rows, 1), 0, top)
    return jnp.take_along_axis(listing, (jnp.arange(top)[None, :] + rotation) % top, axis=1)


def shares(count, total, bound, slope, full):
    weights = [(1 << 20) // math.isqrt(grade ** slope) + 1 for grade in range(1, count + 1)]
    largest = bound if full else min(bound, max(-(-total // count), total * weights[0] // sum(weights)))
    least = 1 if total - largest >= count - 1 else 0
    counts, spare = [largest] + [least] * (count - 1), total - largest - least * (count - 1)
    while spare > 0:
        free = [i for i in range(1, count) if counts[i] < largest] or [i for i in range(1, count) if counts[i] < bound]
        whole, budget = sum([weights[i] for i in free]), spare
        for i in free:
            addition = min(bound - counts[i], max(1, budget * weights[i] // whole), spare)
            counts[i] = counts[i] + addition
            spare = spare - addition
    return np.array(counts)


def centred(key, shape, scale, bound, cuts=(), kind=jnp.bfloat16):
    drawn = scale * jax.random.normal(key, shape, jnp.float32)
    if cuts:
        drawn = drawn * level_of(key, shape, cuts, -0.22, 0.18)
    return jnp.clip(drawn, -bound, bound).astype(kind)


def setup_inputs(seed: int = 0) -> dict:
    key_list = jax.random.split(jax.random.key(seed), 8)
    hot_rows = draw_hot_rows(jax.random.fold_in(key_list[7], 71), 0)
    cold_rows = draw_cold_rows(jax.random.fold_in(key_list[7], 71), 0)
    row_source_keys = jax.random.split(jax.random.fold_in(key_list[2], 1), TOKENS // HOME_TOK)
    row_source_turns = jax.random.permutation(jax.random.fold_in(key_list[2], 3), TOKENS // HOME_TOK)
    row_source = jax.vmap(lambda own, number: shared_out(jax.random.fold_in(key_list[2], 2), own, number, HOME_TOK, 2 * N_TAB, 1, MOST, 2))(row_source_keys, row_source_turns).reshape((TOKENS, 1))
    lengths = draw_lengths(jax.random.fold_in(key_list[7], 71), 0)
    destination = draw_destination(jax.random.fold_in(key_list[7], 71), 0)
    proj_weight = centred(key_list[5], (D, 4 * D), D ** -0.5, 0.1875)
    out_grad = centred(key_list[6], (TOKENS, D), TOKENS ** -0.5, 0.01171875, ((0, 768),))
    return dict(hot_rows=hot_rows, cold_rows=cold_rows, row_source=row_source, lengths=lengths, destination=destination, proj_weight=proj_weight, out_grad=out_grad)


def layer_norm(rows_in):
    center = lax.optimization_barrier(jnp.mean(rows_in, axis=-1, keepdims=True))
    centered = rows_in - center
    deviation = lax.optimization_barrier(jnp.mean(centered * centered, axis=-1, keepdims=True))
    return centered * lax.rsqrt(deviation + 1e-05)

def reference(hot_rows, cold_rows, row_source, lengths, destination, proj_weight, out_grad):
    device_count = N_REP * N_BAL * N_TAB
    code_count = 2 * N_TAB
    row_codes = row_source.reshape(device_count, HOME_TOK)
    code_ids = jnp.arange(code_count, dtype=jnp.int32)
    code_flags = (row_codes[:, :, None] == code_ids[None, None, :]).astype(jnp.int32)
    earlier = jnp.cumsum(code_flags, axis=1, dtype=jnp.int32) - code_flags
    slot_index = lax.optimization_barrier(jnp.sum(earlier * code_flags, axis=2, dtype=jnp.int32))
    device_ids = jnp.arange(device_count, dtype=jnp.int32)[:, None]
    shard_ids = device_ids // N_TAB * N_TAB + row_codes % N_TAB
    buffer_index = (shard_ids * N_TAB + device_ids % N_TAB) * MOST + slot_index
    tier_ids = row_codes // N_TAB

    def home_rows(paired):
        index_row, tier_row = paired
        hot_pick = jnp.take(hot_rows, index_row, axis=0)
        cold_pick = jnp.take(cold_rows, index_row, axis=0).astype(jnp.float32)
        picked = jnp.where(tier_row[:, None] == 0, hot_pick, cold_pick)
        return layer_norm(picked).astype(jnp.bfloat16)
    normed = lax.map(home_rows, (buffer_index, tier_ids))
    flat_normed = normed.reshape(device_count * HOME_TOK, D)
    positions = jnp.arange(HOME_TOK, dtype=jnp.int32)
    scale_factor = HEAD ** (-0.5)
    grad_blocks = out_grad.reshape(device_count, HOME_TOK, D)

    def one_device(total, inputs):
        device, grad_block = inputs
        rep_index = device // (N_BAL * N_TAB)
        bal_index = device // N_TAB % N_BAL
        tab_index = device % N_TAB
        group_len = lengths[rep_index, :, tab_index, :]
        group_dest = destination[rep_index, :, tab_index, :]
        starts = jnp.cumsum(group_len, axis=1, dtype=jnp.int32) - group_len
        arriving = (group_dest == bal_index).astype(jnp.int32)
        in_len = lax.optimization_barrier(jnp.sum(arriving * group_len, axis=1, dtype=jnp.int32))
        in_start = lax.optimization_barrier(jnp.sum(arriving * starts, axis=1, dtype=jnp.int32))
        in_end = jnp.cumsum(in_len, dtype=jnp.int32)
        in_off = in_end - in_len
        segment = lax.optimization_barrier(jnp.sum((in_end[None, :] <= positions[:, None]).astype(jnp.int32), axis=1, dtype=jnp.int32))
        source_device = (rep_index * N_BAL + segment) * N_TAB + tab_index
        source_row = in_start[segment] + positions - in_off[segment]
        balanced = jnp.take(flat_normed, source_device * HOME_TOK + source_row, axis=0)
        projected = jax.nn.silu(jnp.dot(balanced, proj_weight, preferred_element_type=jnp.float32)).astype(jnp.bfloat16)
        gating = projected[:, :D]
        values = projected[:, D:2 * D].reshape(HOME_TOK, HEADS, HEAD)
        queries = projected[:, 2 * D:3 * D].reshape(HOME_TOK, HEADS, HEAD)
        key_rows = projected[:, 3 * D:].reshape(HOME_TOK, HEADS, HEAD)
        scores = jnp.einsum('ihd,jhd->hij', queries.astype(jnp.float32), key_rows.astype(jnp.float32)) * scale_factor
        allowed = (segment[:, None] == segment[None, :]) & (positions[None, :] <= positions[:, None])
        weights = jnp.where(allowed[None], jax.nn.silu(scores), 0.0).astype(jnp.bfloat16)
        attention_sum = jnp.einsum('hij,jhd->ihd', weights.astype(jnp.float32), values.astype(jnp.float32)).reshape(HOME_TOK, D)
        attended = (layer_norm(attention_sum) * gating.astype(jnp.float32)).astype(jnp.bfloat16)
        term = jnp.dot(grad_block.T, attended, preferred_element_type=jnp.float32)
        return (total + term, attended)
    total, attended_all = lax.scan(one_device, jnp.zeros((D, D), jnp.float32), (jnp.arange(device_count, dtype=jnp.int32), grad_blocks))
    return (attended_all.reshape(TOKENS, D), total.astype(jnp.bfloat16))
```

```python
import functools

import jax
import jax.numpy as jnp
from jax import lax
from jax.experimental import pallas as pl
from jax.experimental.pallas import tpu as pltpu
from jax.sharding import PartitionSpec as P

HEAD = 128
MAXLEN = 88
CAP = 96
WIN = 128
F32, BF16 = jnp.float32, jnp.bfloat16
TILE = 128


def iota(shape, dim):
    return lax.broadcasted_iota(jnp.int32, shape, dim)


def normalize(rows_in):
    center = jnp.mean(rows_in, axis=-1, keepdims=True)
    centered = rows_in - center
    deviation = jnp.mean(centered * centered, axis=-1, keepdims=True)
    return centered * lax.rsqrt(deviation + 1e-05)


def dot_nt(a, b):
    return lax.dot_general(a, b, (((1,), (1,)), ((), ())), preferred_element_type=F32)


def dot_nn(a, b):
    return jnp.dot(a, b, preferred_element_type=F32)


def flag(cond):
    return jnp.where(cond, 1.0, 0.0).astype(BF16)


def farthest_first(count):
    return sorted(range(1, count), key=lambda d: -min(d, count - d))


def layer_kernel(
    nr, nb, nt, most, chunks, gchunks,
    hot_hbm, cold_hbm, code_ref, len_ref, dest_ref, w_hbm, og_hbm,
    att_hbm, grad_ref,
    hot, cold, w, og, ogp, xsend, xrecv, bmat, smat, ysend, yrecv, tmat, bal, acc, prj, scale,
    asum, att, csend, crecv, gown, xs2, xr2, ys2, yr2, zs, zr, zo, zg,
    load_sem, xs_sem, xr_sem, ys_sem, yr_sem, cs_sem, cr_sem, xs2_sem, xr2_sem, ys2_sem, yr2_sem,
    zs_sem, zr_sem, gs_sem, gr_sem,
):
    home, model = og.shape
    nx = nt // 2
    width = model // chunks
    gwidth = model // gchunks
    heads = model // HEAD
    pair = 2 * most
    nz = zs.shape[0]
    zwidth = model // nz
    rep_id = lax.axis_index("rep")
    bal_id = lax.axis_index("bal")
    tab_id = lax.axis_index("tab")
    core = lax.rem(tab_id, 2)
    x_id = lax.div(tab_id, 2)

    loads = [
        pltpu.make_async_copy(src, dst, load_sem.at[i])
        for i, (src, dst) in enumerate(
            ((hot_hbm, hot), (cold_hbm, cold), (og_hbm, og), (w_hbm, w))
        )
    ]
    for load in loads:
        load.start()

    barrier = pltpu.get_barrier_semaphore()
    for axis, me, count in (("tab", tab_id, nt), ("bal", bal_id, nb), ("rep", rep_id, nr)):
        for d in range(1, count):
            pl.semaphore_signal(barrier, inc=1, device_id={axis: lax.rem(me + d, count)})

    loads[0].wait()
    loads[1].wait()

    @pl.loop(0, nx)
    def _(i):
        rows = pl.ds(pl.multiple_of(i * 2 * most, 16), 2 * most)
        hot_n = normalize(hot[rows, :])
        cold_n = normalize(cold[rows, :].astype(F32))
        for k in range(2):
            part = slice(k * most, (k + 1) * most)
            block = jnp.concatenate([hot_n[part], cold_n[part]], axis=0).astype(BF16)
            for c in range(chunks):
                xsend[c, 2 * i + k] = block[:, c * width : (c + 1) * width]

    pl.semaphore_wait(barrier, nt - 1 + nb - 1 + nr - 1)

    def x_copy(c, d, arriving):
        p = lax.rem(tab_id + d, nt)
        return pltpu.make_async_remote_copy(
            src_ref=xsend.at[c, p],
            dst_ref=xrecv.at[c, p if arriving else tab_id],
            send_sem=xs_sem.at[c, p],
            recv_sem=xr_sem.at[c, p if arriving else tab_id],
            device_id={"tab": p},
        )

    for c in range(chunks):
        for d in farthest_first(nt):
            x_copy(c, d, False).start()
    for c in range(chunks):
        xrecv[c, tab_id] = xsend[c, tab_id]

    start = [jnp.int32(0)] * nb
    length = [jnp.int32(0)] * nb
    run = jnp.int32(0)
    for h in range(nb):
        here = len_ref[bal_id * nb + h]
        goal = dest_ref[bal_id * nb + h]
        for b in range(nb):
            start[b] = jnp.where(goal == b, run, start[b])
            length[b] = jnp.where(goal == b, here, length[b])
        run = run + here
    in_len, in_off = [], []
    run = jnp.int32(0)
    for s in range(nb):
        got = jnp.int32(0)
        for h in range(nb):
            got = got + jnp.where(dest_ref[s * nb + h] == bal_id, len_ref[s * nb + h], 0)
        in_len.append(got)
        in_off.append(run)
        run = run + got

    codes = code_ref[...]
    flags = jnp.where(iota((2 * nt, home), 0) == codes, 1.0, 0.0)
    before = flag(iota((home, home), 0) < iota((home, home), 1))
    earlier = dot_nn(flags.astype(BF16), before)
    slot = jnp.sum(flags * earlier, axis=0, keepdims=True).astype(jnp.int32)
    tier = jnp.where(codes >= nt, 1, 0)
    place = (codes - nt * tier) * pair + tier * most + slot
    for s in range(nt):
        bmat[s * pair : (s + 1) * pair, :] = flag(iota((pair, home), 0) + s * pair == place)
    offset, position = iota((CAP, home), 0), iota((CAP, home), 1)
    for b in range(nb):
        chosen = flag((position - offset == start[b]) & (offset < length[b]))
        smat[b * CAP : (b + 1) * CAP, :] = dot_nt(chosen, bmat[...]).astype(BF16)
    row, lane = iota((home, WIN), 0), iota((home, WIN), 1)
    for s in range(nb):
        tmat[:, s * WIN : (s + 1) * WIN] = flag((row - in_off[s] == lane) & (lane < in_len[s]))
    yrecv[:, :, CAP:, :] = jnp.zeros((chunks, nb, WIN - CAP, width), BF16)

    def y_copy(c, d, arriving):
        p = lax.rem(bal_id + d, nb)
        at = p if arriving else bal_id
        return pltpu.make_async_remote_copy(
            src_ref=ysend.at[c, p],
            dst_ref=yrecv.at[c, at, pl.ds(0, CAP)],
            send_sem=ys_sem.at[c, p],
            recv_sem=yr_sem.at[c, at],
            device_id={"bal": p},
        )

    for c in range(chunks):
        for d in farthest_first(nt):
            x_copy(c, d, True).wait_recv()
        moved = dot_nn(smat[...], xrecv[c].reshape(nt * pair, width)).astype(BF16)
        ysend[c] = moved.reshape(nb, CAP, width)
        for d in farthest_first(nb):
            y_copy(c, d, False).start()
        yrecv[c, bal_id, 0:CAP] = ysend[c, bal_id]

    loads[2].wait()
    for b in range(nb):
        cols = 16 * nt
        turned = og[:, b * cols : (b + 1) * cols].T
        ogp[:, b * 16 : (b + 1) * 16, :] = turned.reshape(nt, 16, home)
    query, key = iota((TILE, 2 * TILE), 0), iota((TILE, 2 * TILE), 1)
    for i in range(home // TILE):
        at = query + i * TILE
        source = key + (i - 1) * TILE
        first = jnp.zeros_like(at)
        for s in range(1, nb):
            first = jnp.where(in_off[s] <= at, in_off[s], first)
        scale[i] = jnp.where((source <= at) & (source >= first), 0.5 * HEAD**-0.5, 0.0)

    loads[3].wait()
    early = model - width
    step = 512
    for c in range(chunks):
        for d in farthest_first(nb):
            y_copy(c, d, True).wait_recv()
        bal[:, c * width : (c + 1) * width] = dot_nn(
            tmat[...], yrecv[c].reshape(nb * WIN, width)
        ).astype(BF16)
        if c == chunks - 2:

            @pl.loop(0, 4 * model // step)
            def _(n):
                cols = pl.ds(pl.multiple_of(n * step, step), step)
                acc[:, cols] = dot_nn(bal[:, :early], w[:early, cols])

    @pl.loop(0, 4 * model // step)
    def _(n):
        cols = pl.ds(pl.multiple_of(n * step, step), step)
        half = 0.5 * (acc[:, cols] + dot_nn(bal[:, early:], w[early:, cols]))
        prj[:, cols] = (half + half * jnp.tanh(half)).astype(BF16)

    @pl.loop(0, heads)
    def _(h):
        def cols(part):
            return pl.ds(pl.multiple_of(part * model + h * HEAD, HEAD), HEAD)

        for i in range(home // TILE):
            rows = slice(i * TILE, (i + 1) * TILE)
            low = max(0, i - 1) * TILE
            keys = slice(low, (i + 1) * TILE)
            lanes = slice(2 * TILE - (i + 1) * TILE + low, 2 * TILE)
            scores = dot_nt(prj[rows, cols(2)], prj[keys, cols(3)])
            half = scores * scale[i, :, lanes]
            weights = (half + half * jnp.tanh(half)).astype(BF16)
            asum[rows, cols(0)] = dot_nn(weights, prj[keys, cols(1)])

    ln_rows = 64

    @pl.loop(0, home // ln_rows)
    def _(i):
        rows = pl.ds(pl.multiple_of(i * ln_rows, ln_rows), ln_rows)
        att[rows, :] = (normalize(asum[rows, :]) * prj[rows, :model].astype(F32)).astype(BF16)

    att_copy = pltpu.make_async_copy(att, att_hbm, load_sem.at[4])
    att_copy.start()

    def c_copy(g):
        return pltpu.make_async_remote_copy(
            src_ref=csend.at[g],
            dst_ref=crecv.at[g],
            send_sem=cs_sem.at[g],
            recv_sem=cr_sem.at[g],
            device_id={"tab": tab_id + 1 - 2 * core},
        )

    def x2_copy(g, d, arriving):
        p = lax.rem(x_id + d, nx)
        at = p if arriving else x_id
        return pltpu.make_async_remote_copy(
            src_ref=xs2.at[g, p],
            dst_ref=xr2.at[g, at],
            send_sem=xs2_sem.at[g, p],
            recv_sem=xr2_sem.at[g, at],
            device_id={"tab": 2 * p + core},
        )

    def y2_copy(g, d, arriving):
        p = lax.rem(bal_id + d, nb)
        at = p if arriving else bal_id
        return pltpu.make_async_remote_copy(
            src_ref=ys2.at[g, p],
            dst_ref=yr2.at[g, at],
            send_sem=ys2_sem.at[g, p],
            recv_sem=yr2_sem.at[g, at],
            device_id={"bal": p},
        )

    for g in range(gchunks):
        cols = slice(g * gwidth, (g + 1) * gwidth)
        for x in range(nx):
            csend[g, x] = dot_nn(ogp[2 * x + 1 - core], att[:, cols]).astype(BF16)
        c_copy(g).start()
    for g in range(gchunks):
        cols = slice(g * gwidth, (g + 1) * gwidth)
        for x in range(nx):
            gown[g, x] = dot_nn(ogp[2 * x + core], att[:, cols])
    for g in range(gchunks):
        c_copy(g).wait_recv()
        for x in range(nx):
            both = gown[g, x] + crecv[g, x].astype(F32)
            gown[g, x] = both
            xs2[g, x] = both.astype(BF16)
        for d in farthest_first(nx):
            x2_copy(g, d, False).start()
    for g in range(gchunks):
        total = gown[g, x_id]
        for d in farthest_first(nx):
            x2_copy(g, d, True).wait_recv()
            total = total + xr2[g, lax.rem(x_id + d, nx)].astype(F32)
        gown[g, x_id] = total
        ys2[g] = total.astype(BF16).reshape(nb, 16, gwidth)
        for d in farthest_first(nb):
            y2_copy(g, d, False).start()
    for g in range(gchunks):
        own_rows = pl.ds(pl.multiple_of(bal_id * 16, 16), 16)
        total = gown[g, x_id, own_rows, :]
        for d in farthest_first(nb):
            y2_copy(g, d, True).wait_recv()
            total = total + yr2[g, lax.rem(bal_id + d, nb)].astype(F32)
        total = total.astype(BF16)
        for j in range(gwidth // zwidth):
            zs[g * (gwidth // zwidth) + j] = total[:, j * zwidth : (j + 1) * zwidth]

    def z_send(j):
        return pltpu.make_async_remote_copy(
            src_ref=zs.at[j],
            dst_ref=zr.at[rep_id],
            send_sem=zs_sem.at[j],
            recv_sem=zr_sem.at[rep_id],
            device_id={"rep": j},
        )

    def z_arrive(p):
        return pltpu.make_async_remote_copy(
            src_ref=zs.at[0],
            dst_ref=zr.at[p],
            send_sem=zs_sem.at[0],
            recv_sem=zr_sem.at[p],
            device_id={"rep": p},
        )

    def g_send(d):
        p = lax.rem(rep_id + d, nr)
        return pltpu.make_async_remote_copy(
            src_ref=zo,
            dst_ref=zg.at[rep_id],
            send_sem=gs_sem.at[p],
            recv_sem=gr_sem.at[rep_id],
            device_id={"rep": p},
        )

    def g_arrive(j):
        return pltpu.make_async_remote_copy(
            src_ref=zo,
            dst_ref=zg.at[j],
            send_sem=gs_sem.at[0],
            recv_sem=gr_sem.at[j],
            device_id={"rep": j},
        )

    for j in range(nz):

        @pl.when(rep_id != j)
        def _():
            z_send(j).start()

    @pl.when(rep_id < nz)
    def _():
        total = zs[rep_id].astype(F32)
        for d in range(1, nr):
            p = lax.rem(rep_id + d, nr)
            z_arrive(p).wait_recv()
            total = total + zr[p].astype(F32)
        zo[...] = total.astype(BF16)
        for d in farthest_first(nr):
            g_send(d).start()
        zg[rep_id] = total.astype(BF16)

    for j in range(nz):

        @pl.when(rep_id != j)
        def _():
            g_arrive(j).wait_recv()

        grad_ref[:, j * zwidth : (j + 1) * zwidth] = zg[j]

    for c in range(chunks):
        for d in range(1, nt):
            x_copy(c, d, False).wait_send()
        for d in range(1, nb):
            y_copy(c, d, False).wait_send()
    for g in range(gchunks):
        c_copy(g).wait_send()
        for d in range(1, nx):
            x2_copy(g, d, False).wait_send()
        for d in range(1, nb):
            y2_copy(g, d, False).wait_send()
    for j in range(nz):

        @pl.when(rep_id != j)
        def _():
            z_send(j).wait_send()

    @pl.when(rep_id < nz)
    def _():
        for d in range(1, nr):
            g_send(d).wait_send()

    att_copy.wait()


def on_device(sizes, hot_rows, cold_rows, row_source, lengths, destination, proj_weight, out_grad):
    nr, nb, nt = sizes
    home, model = out_grad.shape
    most = hot_rows.shape[0] // nt
    chunks = 4 if model >= 1024 else 2
    gchunks = 2
    nx, width, gwidth, pair = nt // 2, model // chunks, model // gchunks, 2 * most
    nz = min(nr, 8)
    vmem = pltpu.VMEM
    dma = pltpu.SemaphoreType.DMA
    scratch = [
        vmem(hot_rows.shape, F32),
        vmem(cold_rows.shape, BF16),
        vmem(proj_weight.shape, BF16),
        vmem(out_grad.shape, BF16),
        vmem((nt, nb * 16, home), BF16),
        vmem((chunks, nt, pair, width), BF16),
        vmem((chunks, nt, pair, width), BF16),
        vmem((nt * pair, home), BF16),
        vmem((nb * CAP, nt * pair), BF16),
        vmem((chunks, nb, CAP, width), BF16),
        vmem((chunks, nb, WIN, width), BF16),
        vmem((home, nb * WIN), BF16),
        vmem((home, model), BF16),
        vmem((home, 4 * model), F32),
        vmem((home, 4 * model), BF16),
        vmem((home // TILE, TILE, 2 * TILE), F32),
        vmem((home, model), F32),
        vmem((home, model), BF16),
        vmem((gchunks, nx, nb * 16, gwidth), BF16),
        vmem((gchunks, nx, nb * 16, gwidth), BF16),
        vmem((gchunks, nx, nb * 16, gwidth), F32),
        vmem((gchunks, nx, nb * 16, gwidth), BF16),
        vmem((gchunks, nx, nb * 16, gwidth), BF16),
        vmem((gchunks, nb, 16, gwidth), BF16),
        vmem((gchunks, nb, 16, gwidth), BF16),
        vmem((nz, 16, model // nz), BF16),
        vmem((nr, 16, model // nz), BF16),
        vmem((16, model // nz), BF16),
        vmem((nz, 16, model // nz), BF16),
        dma((5,)),
        dma((chunks, nt)),
        dma((chunks, nt)),
        dma((chunks, nb)),
        dma((chunks, nb)),
        dma((gchunks,)),
        dma((gchunks,)),
        dma((gchunks, nx)),
        dma((gchunks, nx)),
        dma((gchunks, nb)),
        dma((gchunks, nb)),
        dma((nz,)),
        dma((nr,)),
        dma((nr,)),
        dma((nz,)),
    ]
    hbm = pl.BlockSpec(memory_space=pl.ANY)
    here = pl.BlockSpec(memory_space=pltpu.VMEM)
    scalar = pl.BlockSpec(memory_space=pltpu.SMEM)
    return pl.pallas_call(
        functools.partial(layer_kernel, nr, nb, nt, most, chunks, gchunks),
        out_shape=(
            jax.ShapeDtypeStruct((home, model), BF16),
            jax.ShapeDtypeStruct((model // (nb * nt), model), BF16),
        ),
        in_specs=[hbm, hbm, here, scalar, scalar, hbm, hbm],
        out_specs=(hbm, here),
        scratch_shapes=scratch,
        compiler_params=pltpu.CompilerParams(
            collective_id=0, has_side_effects=True, vmem_limit_bytes=58 * 1024 * 1024
        ),
    )(
        hot_rows,
        cold_rows,
        row_source.reshape(1, home),
        lengths.reshape(-1),
        destination.reshape(-1),
        proj_weight,
        out_grad,
    )


def solution(mesh):
    sizes = tuple(mesh.shape[axis] for axis in ("rep", "bal", "tab"))
    in_specs = (
        P(("rep", "bal", "tab"), None),
        P(("rep", "bal", "tab"), None),
        P(("rep", "bal", "tab"), None),
        P("rep", None, "tab", None),
        P("rep", None, "tab", None),
        P(),
        P(("rep", "bal", "tab"), None),
    )
    out_specs = (P(("rep", "bal", "tab"), None), P(("bal", "tab"), None))
    return jax.shard_map(
        functools.partial(on_device, sizes),
        mesh=mesh,
        in_specs=in_specs,
        out_specs=out_specs,
        check_vma=False,
    )
```

```python
import functools

import jax
import jax.numpy as jnp
from jax import lax
from jax.experimental import pallas as pl
from jax.experimental.pallas import tpu as pltpu
from jax.sharding import PartitionSpec as P

HEAD = 128
MAXLEN = 88
WIN = 96
F32, BF16 = jnp.float32, jnp.bfloat16
TILE = 128


def iota(shape, dim):
    return lax.broadcasted_iota(jnp.int32, shape, dim)


def normalize(rows_in):
    center = jnp.mean(rows_in, axis=-1, keepdims=True)
    centered = rows_in - center
    deviation = jnp.mean(centered * centered, axis=-1, keepdims=True)
    return centered * lax.rsqrt(deviation + 1e-05)


def dot_nt(a, b):
    return lax.dot_general(a, b, (((1,), (1,)), ((), ())), preferred_element_type=F32)


def dot_nn(a, b):
    return jnp.dot(a, b, preferred_element_type=F32)


def flag(cond):
    return jnp.where(cond, 1.0, 0.0).astype(BF16)


def farthest_first(count):
    return sorted(range(1, count), key=lambda d: -min(d, count - d))


def layer_kernel(
    nr, nb, nt, most, widths, ahead, gorder,
    hot_hbm, cold_hbm, code_hbm, len_hbm, dest_hbm, w_hbm, og_hbm,
    att_hbm, grad_ref,
    xsend, xrecv, ysend, yrecv,
    code_ref, len_ref, dest_ref,
    hot, cold, w, og, ogp, ogr, bmat, smat, spread, tmat, bal, acc, prj, scale,
    asum, att, attr, gown, xs2, xr2, ys2, yr2, ybs, ybr, xbs, xbr, zs, zr, zo, zg,
    load_sem, xs_sem, xr_sem, ys_sem, yr_sem, os_sem, or_sem, as_sem, ar_sem,
    xs2_sem, xr2_sem, ys2_sem, yr2_sem, ybs_sem, ybr_sem, xbs_sem, xbr_sem,
    zs_sem, zr_sem, gs_sem, gr_sem,
):
    home, model = og.shape
    nx = nt // 2
    chunks = len(widths)
    firsts = [sum(widths[:c]) for c in range(chunks)]
    tiles = home // TILE
    heads = model // HEAD
    pair = 2 * most
    nz = zs.shape[0]
    zwidth = model // nz
    gwidth = model // len(gorder)
    rep_id = lax.axis_index("rep")
    bal_id = lax.axis_index("bal")
    tab_id = lax.axis_index("tab")
    core = lax.rem(tab_id, 2)
    x_id = lax.div(tab_id, 2)
    sibling = tab_id + 1 - 2 * core

    loads = [
        pltpu.make_async_copy(src, dst, load_sem.at[i])
        for i, (src, dst) in enumerate(
            (
                (hot_hbm, hot), (cold_hbm, cold), (code_hbm, code_ref), (len_hbm, len_ref),
                (dest_hbm, dest_ref), (og_hbm, og), (w_hbm, w),
            )
        )
    ]
    att_copy = pltpu.make_async_copy(att, att_hbm, load_sem.at[7])

    def remote(src, dst, send, recv, axis, peer):
        return pltpu.make_async_remote_copy(
            src_ref=src, dst_ref=dst, send_sem=send, recv_sem=recv, device_id={axis: peer}
        )

    def exchange(src, dst, send, recv, axis, me, count, d, c, arriving):
        p = lax.rem(me + d, count)
        at = p if arriving else me
        peer = 2 * p + core if axis == "x" else p
        return remote(
            src.at[p], dst.at[at], send.at[c, p], recv.at[c, at], "tab" if axis == "x" else axis, peer
        )

    def x_copy(c, d, arriving=False):
        return exchange(xsend[c], xrecv[c], xs_sem, xr_sem, "tab", tab_id, nt, d, c, arriving)

    def y_copy(c, d, arriving=False):
        return exchange(ysend[c], yrecv[c], ys_sem, yr_sem, "bal", bal_id, nb, d, c, arriving)

    def x2_copy(a, d, arriving=False):
        return exchange(
            xs2.at[a], xr2.at[a], xs2_sem, xr2_sem, "x", x_id, nx, d, a, arriving
        )

    def y2_copy(a, d, arriving=False):
        return exchange(
            ys2.at[a], yr2.at[a], ys2_sem, yr2_sem, "bal", bal_id, nb, d, a, arriving
        )

    def yb_copy(a, d, arriving=False):
        return exchange(
            ybs.at[a], ybr.at[a], ybs_sem, ybr_sem, "bal", bal_id, nb, d, a, arriving
        )

    def xb_copy(a, d, arriving=False):
        return exchange(
            xbs.at[a], xbr.at[a], xbs_sem, xbr_sem, "x", x_id, nx, d, a, arriving
        )

    def o_copy(x):
        return remote(
            ogp.at[2 * x + 1 - core], ogr.at[x], os_sem.at[x], or_sem.at[x], "tab", sibling
        )

    def a_copy(i):
        rows = pl.ds(i * TILE, TILE)
        return remote(att.at[rows], attr.at[rows], as_sem.at[i], ar_sem.at[i], "tab", sibling)

    def z_copy(j):
        return remote(zs.at[j], zr.at[rep_id], zs_sem.at[j], zr_sem.at[rep_id], "rep", j)

    def z_arrive(p):
        return remote(zs.at[0], zr.at[p], zs_sem.at[0], zr_sem.at[p], "rep", p)

    def g_copy(d):
        p = lax.rem(rep_id + d, nr)
        return remote(zo, zg.at[rep_id], gs_sem.at[p], gr_sem.at[rep_id], "rep", p)

    def g_arrive(j):
        return remote(zo, zg.at[j], gs_sem.at[0], gr_sem.at[j], "rep", j)

    def load_and_greet():
        for load in loads[:5]:
            load.start()
        barrier = pltpu.get_barrier_semaphore()
        for axis, me, count in (("tab", tab_id, nt), ("bal", bal_id, nb), ("rep", rep_id, nr)):
            for d in range(1, count):
                pl.semaphore_signal(barrier, inc=1, device_id={axis: lax.rem(me + d, count)})
        loads[0].wait()
        loads[1].wait()
        loads[5].start()
        loads[6].start()

    def normalize_rows():
        @pl.loop(0, nx)
        def _(i):
            rows = pl.ds(pl.multiple_of(i * 2 * most, 16), 2 * most)
            hot_n = normalize(hot[rows, :])
            cold_n = normalize(cold[rows, :].astype(F32))
            for k in range(2):
                part = slice(k * most, (k + 1) * most)
                block = jnp.concatenate([hot_n[part], cold_n[part]], axis=0).astype(BF16)
                for c in range(chunks):
                    xsend[c][2 * i + k] = block[:, firsts[c] : firsts[c] + widths[c]]

    def greeted():
        pl.semaphore_wait(pltpu.get_barrier_semaphore(), nt - 1 + nb - 1 + nr - 1)

    def x_start(c):
        for d in farthest_first(nt):
            x_copy(c, d).start()

    def history_bounds():
        for load in loads[2:5]:
            load.wait()
        start = [jnp.int32(0)] * nb
        length = [jnp.int32(0)] * nb
        run = jnp.int32(0)
        for h in range(nb):
            here = len_ref[0, bal_id, 0, h]
            goal = dest_ref[0, bal_id, 0, h]
            for b in range(nb):
                start[b] = jnp.where(goal == b, run, start[b])
                length[b] = jnp.where(goal == b, here, length[b])
            run = run + here
        in_off = []
        run = jnp.int32(0)
        for s in range(nb):
            in_off.append(run)
            for h in range(nb):
                run = run + jnp.where(dest_ref[0, s, 0, h] == bal_id, len_ref[0, s, 0, h], 0)
        return start, length, in_off

    def placements(start, length, in_off):
        codes = code_ref[...]
        flags = jnp.where(iota((2 * nt, home), 0) == codes, 1.0, 0.0)
        before = flag(iota((home, home), 0) < iota((home, home), 1))
        earlier = dot_nn(flags.astype(BF16), before)
        slot = jnp.sum(flags * earlier, axis=0, keepdims=True).astype(jnp.int32)
        tier = jnp.where(codes >= nt, 1, 0)
        place = (codes - nt * tier) * pair + tier * most + slot
        bmat[...] = flag(iota((nt * pair, home), 0) == place)
        gap = iota((MAXLEN, home), 1) - iota((MAXLEN, home), 0)
        offset = iota((MAXLEN, home), 0)
        for b in range(0, nb, 2):
            chosen = jnp.concatenate(
                [
                    jnp.where((gap == start[k]) & (offset < length[k]), 1.0, 0.0)
                    for k in (b, b + 1)
                ],
                axis=0,
            ).astype(BF16)
            smat[b * MAXLEN : (b + 2) * MAXLEN, :] = dot_nt(chosen, bmat[...]).astype(BF16)
        row = iota((home, WIN), 0)
        moved = jnp.zeros_like(row)
        for s in range(1, nb):
            moved = jnp.where(row >= in_off[s], s * WIN - in_off[s], moved)
        source = (row + moved)[:, :1]
        tmat[...] = flag(iota((home, nb * WIN), 1) == source)

    def x_to_y(c):
        for d in farthest_first(nt):
            x_copy(c, d, True).wait_recv()
        if c + ahead < chunks:
            x_start(c + ahead)
        xrecv[c][tab_id] = xsend[c][tab_id]
        width = widths[c]
        out = dot_nn(smat[...], xrecv[c][...].reshape(nt * pair, width))
        for b in range(nb):
            block = out[b * MAXLEN : (b + 1) * MAXLEN]
            if width > 128:
                block = jnp.concatenate([block[:, : width // 2], block[:, width // 2 :]], axis=0)
            else:
                block = jnp.concatenate([block, jnp.zeros((WIN - MAXLEN, width), F32)], axis=0)
            ysend[c][b] = block.astype(BF16)
        for d in farthest_first(nb):
            y_copy(c, d).start()
        yrecv[c][bal_id] = ysend[c][bal_id]

    def y_in(c):
        width = widths[c]
        for d in farthest_first(nb):
            y_copy(c, d, True).wait_recv()
        if width > 128:
            for s in range(nb):
                block = yrecv[c][s].astype(F32)
                block = jnp.concatenate([block[:MAXLEN], block[MAXLEN:]], axis=1)
                block = jnp.concatenate([block, jnp.zeros((WIN - MAXLEN, width), F32)], axis=0)
                spread[s * WIN : (s + 1) * WIN, :width] = block.astype(BF16)
            arrived = spread[:, :width]
        else:
            arrived = yrecv[c][...].reshape(nb * WIN, width)
        bal[:, firsts[c] : firsts[c] + width] = dot_nn(tmat[...], arrived).astype(BF16)

    def turn_out_grad():
        loads[5].wait()
        for b in range(nb):
            cols = 16 * nt
            turned = og[:, b * cols : (b + 1) * cols].T
            ogp[:, b * 16 : (b + 1) * 16, :] = turned.reshape(nt, 16, home)
        for x in range(nx):
            o_copy(x).start()

    def mask_scale(in_off):
        query, key = iota((TILE, 2 * TILE), 0), iota((TILE, 2 * TILE), 1)
        for i in range(tiles):
            at = query + i * TILE
            source = key + (i - 1) * TILE
            first = jnp.zeros_like(at)
            for s in range(1, nb):
                first = jnp.where(in_off[s] <= at, in_off[s], first)
            scale[i] = jnp.where((source <= at) & (source >= first), 0.5 * HEAD**-0.5, 0.0)

    step = 512
    early = firsts[-1]

    def project_early():
        loads[6].wait()

        @pl.loop(0, 4 * model // step)
        def _(n):
            cols = pl.ds(pl.multiple_of(n * step, step), step)
            acc[:, cols] = dot_nn(bal[:, :early], w[:early, cols])

    def project_late():
        @pl.loop(0, 4 * model // step)
        def _(n):
            cols = pl.ds(pl.multiple_of(n * step, step), step)
            half = 0.5 * (acc[:, cols] + dot_nn(bal[:, early:], w[early:, cols]))
            prj[:, cols] = (half + half * jnp.tanh(half)).astype(BF16)

    def attend(i):
        rows = slice(i * TILE, (i + 1) * TILE)
        low = max(0, i - 1) * TILE
        keys = slice(low, (i + 1) * TILE)
        lanes = slice(2 * TILE - (i + 1) * TILE + low, 2 * TILE)

        @pl.loop(0, heads // 2)
        def _(pair_of_heads):
            for k in range(2):
                def cols(part):
                    at = part * model + (pair_of_heads * 2 + k) * HEAD
                    return pl.ds(pl.multiple_of(at, HEAD), HEAD)

                scores = dot_nt(prj[rows, cols(2)], prj[keys, cols(3)])
                half = scores * scale[i, :, lanes]
                weights = (half + half * jnp.tanh(half)).astype(BF16)
                asum[rows, cols(0)] = dot_nn(weights, prj[keys, cols(1)])

    def gate(i):
        rows = slice(i * TILE, (i + 1) * TILE)
        att[rows, :] = (normalize(asum[rows, :]) * prj[rows, :model].astype(F32)).astype(BF16)

    def partial(x, cols):
        return dot_nn(ogp[2 * x + core], att[:, cols]) + dot_nn(ogr[x], attr[:, cols])

    def columns(g):
        return slice(g * gwidth, (g + 1) * gwidth)

    groups = []
    for g, kind in enumerate(gorder):
        groups.append((kind, gorder[:g].count(kind)))

    def grad_start(g):
        kind, a = groups[g]
        if kind == "A":
            for d in farthest_first(nx) + [0]:
                x = lax.rem(x_id + d, nx)
                part = partial(x, columns(g))
                if d:
                    xs2[a, x] = part.astype(BF16)
                    x2_copy(a, d).start()
                else:
                    gown[a] = part
        else:
            for x in range(nx):
                part = partial(x, columns(g)).astype(BF16)
                ybs[a, :, x * 16 : (x + 1) * 16, :] = part.reshape(nb, 16, gwidth)
            for d in farthest_first(nb):
                yb_copy(a, d).start()

    def grad_turn(g):
        kind, a = groups[g]
        if kind == "A":
            total = gown[a]
            for d in farthest_first(nx):
                x2_copy(a, d, True).wait_recv()
                total = total + xr2[a, lax.rem(x_id + d, nx)].astype(F32)
            ys2[a] = total.astype(BF16).reshape(nb, 16, gwidth)
            for d in farthest_first(nb):
                y2_copy(a, d).start()
        else:
            total = ybs[a, bal_id].astype(F32)
            for d in farthest_first(nb):
                yb_copy(a, d, True).wait_recv()
                total = total + ybr[a, lax.rem(bal_id + d, nb)].astype(F32)
            xbs[a] = total.astype(BF16).reshape(nx, 16, gwidth)
            for d in farthest_first(nx):
                xb_copy(a, d).start()

    def grad_end(g):
        kind, a = groups[g]
        if kind == "A":
            total = ys2[a, bal_id].astype(F32)
            for d in farthest_first(nb):
                y2_copy(a, d, True).wait_recv()
                total = total + yr2[a, lax.rem(bal_id + d, nb)].astype(F32)
        else:
            total = xbs[a, x_id].astype(F32)
            for d in farthest_first(nx):
                xb_copy(a, d, True).wait_recv()
                total = total + xbr[a, lax.rem(x_id + d, nx)].astype(F32)
        total = total.astype(BF16)
        for k in range(gwidth // zwidth):
            j = g * (gwidth // zwidth) + k
            zs[j] = total[:, k * zwidth : (k + 1) * zwidth]

            @pl.when(rep_id != j)
            def _():
                z_copy(j).start()

    def grad_spread():
        @pl.when(rep_id < nz)
        def _():
            total = zs[rep_id].astype(F32)
            for d in range(1, nr):
                p = lax.rem(rep_id + d, nr)
                z_arrive(p).wait_recv()
                total = total + zr[p].astype(F32)
            zo[...] = total.astype(BF16)
            for d in farthest_first(nr):
                g_copy(d).start()
            zg[rep_id] = total.astype(BF16)

        for j in range(nz):

            @pl.when(rep_id != j)
            def _():
                g_arrive(j).wait_recv()

            grad_ref[:, j * zwidth : (j + 1) * zwidth] = zg[j]

    def all_sent():
        for c in range(chunks):
            for d in range(1, nt):
                x_copy(c, d).wait_send()
            for d in range(1, nb):
                y_copy(c, d).wait_send()
        for x in range(nx):
            o_copy(x).wait_send()
        for i in range(tiles):
            a_copy(i).wait_send()
        for kind, a in groups:
            for d in range(1, nx):
                (x2_copy if kind == "A" else xb_copy)(a, d).wait_send()
            for d in range(1, nb):
                (y2_copy if kind == "A" else yb_copy)(a, d).wait_send()
        for j in range(nz):

            @pl.when(rep_id != j)
            def _():
                z_copy(j).wait_send()

        @pl.when(rep_id < nz)
        def _():
            for d in range(1, nr):
                g_copy(d).wait_send()

    load_and_greet()
    normalize_rows()
    greeted()
    for c in range(min(ahead, chunks)):
        x_start(c)
    start, length, in_off = history_bounds()
    placements(start, length, in_off)
    for c in range(chunks):
        x_to_y(c)
    turn_out_grad()
    mask_scale(in_off)
    for c in range(chunks - 1):
        y_in(c)
    project_early()
    y_in(chunks - 1)
    project_late()
    for i in range(tiles):
        attend(i)
        gate(i)
        a_copy(i).start()
    att_copy.start()
    for x in range(nx):
        o_copy(x).wait_recv()
    for i in range(tiles):
        a_copy(i).wait_recv()
    for g in range(len(gorder)):
        grad_start(g)
    for g in range(len(gorder)):
        grad_turn(g)
    for g in range(len(gorder)):
        grad_end(g)
    grad_spread()
    all_sent()
    att_copy.wait()


def on_device(sizes, hot_rows, cold_rows, row_source, lengths, destination, proj_weight, out_grad):
    nr, nb, nt = sizes
    home, model = out_grad.shape
    most = hot_rows.shape[0] // nt
    widths = (128, 256, 256, 256, 128)
    ahead = 2
    gorder = "BAAA"
    chunks, groups = len(widths), len(gorder)
    acount, bcount = gorder.count("A"), gorder.count("B")
    nx, gwidth, pair = nt // 2, model // groups, 2 * most
    nz = min(nr, 8)
    vmem = pltpu.VMEM
    dma = pltpu.SemaphoreType.DMA

    def y_block(width):
        return (2 * MAXLEN, width // 2) if width > 128 else (WIN, width)

    x_parts = [vmem((nt, pair, width), BF16) for width in widths]
    y_parts = [vmem((nb, *y_block(width)), BF16) for width in widths]
    scratch = [
        x_parts,
        x_parts,
        y_parts,
        y_parts,
        vmem((1, home), jnp.int32),
        pltpu.SMEM(lengths.shape, jnp.int32),
        pltpu.SMEM(destination.shape, jnp.int32),
        vmem(hot_rows.shape, F32),
        vmem(cold_rows.shape, BF16),
        vmem(proj_weight.shape, BF16),
        vmem(out_grad.shape, BF16),
        vmem((nt, nb * 16, home), BF16),
        vmem((nx, nb * 16, home), BF16),
        vmem((nt * pair, home), BF16),
        vmem((nb * MAXLEN, nt * pair), BF16),
        vmem((nb * WIN, max(widths)), BF16),
        vmem((home, nb * WIN), BF16),
        vmem((home, model), BF16),
        vmem((home, 4 * model), F32),
        vmem((home, 4 * model), BF16),
        vmem((home // TILE, TILE, 2 * TILE), F32),
        vmem((home, model), F32),
        vmem((home, model), BF16),
        vmem((home, model), BF16),
        vmem((acount, nb * 16, gwidth), F32),
        vmem((acount, nx, nb * 16, gwidth), BF16),
        vmem((acount, nx, nb * 16, gwidth), BF16),
        vmem((acount, nb, 16, gwidth), BF16),
        vmem((acount, nb, 16, gwidth), BF16),
        vmem((bcount, nb, nx * 16, gwidth), BF16),
        vmem((bcount, nb, nx * 16, gwidth), BF16),
        vmem((bcount, nx, 16, gwidth), BF16),
        vmem((bcount, nx, 16, gwidth), BF16),
        vmem((nz, 16, model // nz), BF16),
        vmem((nr, 16, model // nz), BF16),
        vmem((16, model // nz), BF16),
        vmem((nz, 16, model // nz), BF16),
        dma((8,)),
        dma((chunks, nt)),
        dma((chunks, nt)),
        dma((chunks, nb)),
        dma((chunks, nb)),
        dma((nx,)),
        dma((nx,)),
        dma((home // TILE,)),
        dma((home // TILE,)),
        dma((acount, nx)),
        dma((acount, nx)),
        dma((acount, nb)),
        dma((acount, nb)),
        dma((bcount, nb)),
        dma((bcount, nb)),
        dma((bcount, nx)),
        dma((bcount, nx)),
        dma((nz,)),
        dma((nr,)),
        dma((nr,)),
        dma((nz,)),
    ]
    hbm = pl.BlockSpec(memory_space=pl.ANY)
    return pl.pallas_call(
        functools.partial(layer_kernel, nr, nb, nt, most, widths, ahead, gorder),
        out_shape=(
            jax.ShapeDtypeStruct((home, model), BF16),
            jax.ShapeDtypeStruct((model // (nb * nt), model), BF16),
        ),
        in_specs=[hbm] * 7,
        out_specs=(hbm, pl.BlockSpec(memory_space=pltpu.VMEM)),
        scratch_shapes=scratch,
        compiler_params=pltpu.CompilerParams(
            collective_id=0, has_side_effects=True, vmem_limit_bytes=58 * 1024 * 1024
        ),
    )(
        hot_rows,
        cold_rows,
        row_source.reshape(1, home),
        lengths,
        destination,
        proj_weight,
        out_grad,
    )


def solution(mesh):
    sizes = tuple(mesh.shape[axis] for axis in ("rep", "bal", "tab"))
    in_specs = (
        P(("rep", "bal", "tab"), None),
        P(("rep", "bal", "tab"), None),
        P(("rep", "bal", "tab"), None),
        P("rep", None, "tab", None),
        P("rep", None, "tab", None),
        P(),
        P(("rep", "bal", "tab"), None),
    )
    out_specs = (P(("rep", "bal", "tab"), None), P(("bal", "tab"), None))
    return jax.shard_map(
        functools.partial(on_device, sizes),
        mesh=mesh,
        in_specs=in_specs,
        out_specs=out_specs,
        check_vma=False,
    )
```

```python
import functools

import jax
import jax.numpy as jnp
from jax import lax
from jax.experimental import pallas as pl
from jax.experimental.pallas import tpu as pltpu
from jax.sharding import PartitionSpec as P

HEAD = 128
MAXLEN = 88
WIN = 96
F32, BF16 = jnp.float32, jnp.bfloat16
TILE = 128


def iota(shape, dim):
    return lax.broadcasted_iota(jnp.int32, shape, dim)


def normalize(rows_in):
    center = jnp.mean(rows_in, axis=-1, keepdims=True)
    centered = rows_in - center
    deviation = jnp.mean(centered * centered, axis=-1, keepdims=True)
    return centered * lax.rsqrt(deviation + 1e-05)


def dot_nt(a, b):
    return lax.dot_general(a, b, (((1,), (1,)), ((), ())), preferred_element_type=F32)


def dot_nn(a, b):
    return jnp.dot(a, b, preferred_element_type=F32)


def flag(cond):
    return jnp.where(cond, 1.0, 0.0).astype(BF16)


def farthest_first(count):
    return sorted(range(1, count), key=lambda d: -min(d, count - d))


def layer_kernel(
    nr, nb, nt, most, widths, ahead, groups,
    hot_hbm, cold_hbm, code_hbm, len_hbm, dest_hbm, w_hbm, og_hbm,
    att_hbm, grad_ref,
    xsend, xrecv, ysend, yrecv, first_out, first_in, next_out, next_in, whole_out, whole_in,
    code_ref, len_ref, dest_ref,
    hot, cold, w, og, ogp, ogr, bmat, smat, spread, tmat, bal, acc, prj, scale,
    asum, att, attr, zs, zr, zo, zg,
    load_sem, xs_sem, xr_sem, ys_sem, yr_sem, os_sem, or_sem, as_sem, ar_sem,
    fs_sem, fr_sem, ns_sem, nr_sem, ws_sem, wr_sem, zs_sem, zr_sem, gs_sem, gr_sem, hop_sem,
):
    home, model = og.shape
    nx = nt // 2
    chunks = len(widths)
    firsts = [sum(widths[:c]) for c in range(chunks)]
    tiles = home // TILE
    heads = model // HEAD
    pair = 2 * most
    gcount = len(groups)
    gfirsts = [sum(width for _, width, _ in groups[:g]) for g in range(gcount)]
    direct = [g for g in range(gcount) if groups[g][2]]
    owned = [
        (g, k) for g in range(gcount) if not groups[g][2] for k in range(groups[g][1] // TILE)
    ]
    nz = len(owned)
    rep_id = lax.axis_index("rep")
    bal_id = lax.axis_index("bal")
    tab_id = lax.axis_index("tab")
    core = lax.rem(tab_id, 2)
    x_id = lax.div(tab_id, 2)
    sibling = tab_id + 1 - 2 * core

    loads = [
        pltpu.make_async_copy(src, dst, load_sem.at[i])
        for i, (src, dst) in enumerate(
            (
                (hot_hbm, hot), (cold_hbm, cold), (code_hbm, code_ref), (len_hbm, len_ref),
                (dest_hbm, dest_ref), (og_hbm, og), (w_hbm, w),
            )
        )
    ]
    att_copy = pltpu.make_async_copy(att, att_hbm, load_sem.at[7])

    def remote(src, dst, send, recv, axis, peer):
        return pltpu.make_async_remote_copy(
            src_ref=src, dst_ref=dst, send_sem=send, recv_sem=recv, device_id={axis: peer}
        )

    def exchange(src, dst, send, recv, axis, me, count, d, c, arriving):
        p = lax.rem(me + d, count)
        at = p if arriving else me
        peer = 2 * p + core if axis == "x" else p
        return remote(
            src.at[p], dst.at[at], send.at[c, p], recv.at[c, at], "tab" if axis == "x" else axis, peer
        )

    def x_copy(c, d, arriving=False):
        return exchange(xsend[c], xrecv[c], xs_sem, xr_sem, "tab", tab_id, nt, d, c, arriving)

    def y_copy(c, d, arriving=False):
        return exchange(ysend[c], yrecv[c], ys_sem, yr_sem, "bal", bal_id, nb, d, c, arriving)

    def over(axis):
        return ("x", x_id, nx) if axis == "x" else ("bal", bal_id, nb)

    def first_copy(g, d, arriving=False):
        axis = over(groups[g][0][0])
        return exchange(first_out[g], first_in[g], fs_sem, fr_sem, *axis, d, g, arriving)

    def next_copy(g, d, arriving=False):
        axis = over(groups[g][0][1])
        return exchange(next_out[g], next_in[g], ns_sem, nr_sem, *axis, d, g, arriving)

    def whole_copy(k, d, arriving=False):
        p = lax.rem(rep_id + d, nr)
        at = p if arriving else rep_id
        return remote(
            whole_out[k], whole_in[k].at[at], ws_sem.at[k, p], wr_sem.at[k, at], "rep", p
        )

    def o_copy(x):
        return remote(
            ogp.at[2 * x + 1 - core], ogr.at[x], os_sem.at[x], or_sem.at[x], "tab", sibling
        )

    def a_copy(i):
        rows = pl.ds(i * TILE, TILE)
        return remote(att.at[rows], attr.at[rows], as_sem.at[i], ar_sem.at[i], "tab", sibling)

    def z_copy(j):
        return remote(zs.at[j], zr.at[rep_id], zs_sem.at[j], zr_sem.at[rep_id], "rep", j)

    def z_arrive(p):
        return remote(zs.at[0], zr.at[p], zs_sem.at[0], zr_sem.at[p], "rep", p)

    def g_copy(d):
        p = lax.rem(rep_id + d, nr)
        return remote(zo, zg.at[rep_id], gs_sem.at[p], gr_sem.at[rep_id], "rep", p)

    def g_arrive(j):
        return remote(zo, zg.at[j], gs_sem.at[0], gr_sem.at[j], "rep", j)

    def load_and_greet():
        for load in loads[:5]:
            load.start()
        barrier = pltpu.get_barrier_semaphore()
        for axis, me, count, reach in (
            ("tab", tab_id, nt, range(1, nt)),
            ("bal", bal_id, nb, range(1, nb)),
            ("rep", rep_id, nr, (1, nr - 1)),
        ):
            for d in reach:
                pl.semaphore_signal(barrier, inc=1, device_id={axis: lax.rem(me + d, count)})
        loads[0].wait()
        loads[1].wait()
        loads[5].start()
        loads[6].start()

    def normalize_rows():
        @pl.loop(0, nx)
        def _(i):
            rows = pl.ds(pl.multiple_of(i * 2 * most, 16), 2 * most)
            hot_n = normalize(hot[rows, :])
            cold_n = normalize(cold[rows, :].astype(F32))
            for k in range(2):
                part = slice(k * most, (k + 1) * most)
                block = jnp.concatenate([hot_n[part], cold_n[part]], axis=0).astype(BF16)
                for c in range(chunks):
                    xsend[c][2 * i + k] = block[:, firsts[c] : firsts[c] + widths[c]]

    def greeted():
        pl.semaphore_wait(pltpu.get_barrier_semaphore(), nt - 1 + nb - 1 + 2)

    hops = nr // 2 - 1

    def hop_signal(k):
        for side in range(2):
            peer = lax.rem(rep_id + (nr - 1 if side else 1), nr)
            pl.semaphore_signal(hop_sem.at[k, side], inc=1, device_id={"rep": peer})

    def hop_wait(k):
        for side in range(2):
            pl.semaphore_wait(hop_sem.at[k, side], 1)

    def x_start(c):
        for d in farthest_first(nt):
            x_copy(c, d).start()

    def history_bounds():
        for load in loads[2:5]:
            load.wait()
        start = [jnp.int32(0)] * nb
        length = [jnp.int32(0)] * nb
        run = jnp.int32(0)
        for h in range(nb):
            here = len_ref[0, bal_id, 0, h]
            goal = dest_ref[0, bal_id, 0, h]
            for b in range(nb):
                start[b] = jnp.where(goal == b, run, start[b])
                length[b] = jnp.where(goal == b, here, length[b])
            run = run + here
        in_off = []
        run = jnp.int32(0)
        for s in range(nb):
            in_off.append(run)
            for h in range(nb):
                run = run + jnp.where(dest_ref[0, s, 0, h] == bal_id, len_ref[0, s, 0, h], 0)
        return start, length, in_off

    def placements(start, length, in_off):
        codes = code_ref[...]
        flags = jnp.where(iota((2 * nt, home), 0) == codes, 1.0, 0.0)
        before = flag(iota((home, home), 0) < iota((home, home), 1))
        earlier = dot_nn(flags.astype(BF16), before)
        slot = jnp.sum(flags * earlier, axis=0, keepdims=True).astype(jnp.int32)
        tier = jnp.where(codes >= nt, 1, 0)
        place = (codes - nt * tier) * pair + tier * most + slot
        bmat[...] = flag(iota((nt * pair, home), 0) == place)
        gap = iota((MAXLEN, home), 1) - iota((MAXLEN, home), 0)
        offset = iota((MAXLEN, home), 0)
        for b in range(0, nb, 2):
            chosen = jnp.concatenate(
                [
                    jnp.where((gap == start[k]) & (offset < length[k]), 1.0, 0.0)
                    for k in (b, b + 1)
                ],
                axis=0,
            ).astype(BF16)
            smat[b * MAXLEN : (b + 2) * MAXLEN, :] = dot_nt(chosen, bmat[...]).astype(BF16)
        row = iota((home, WIN), 0)
        moved = jnp.zeros_like(row)
        for s in range(1, nb):
            moved = jnp.where(row >= in_off[s], s * WIN - in_off[s], moved)
        source = (row + moved)[:, :1]
        tmat[...] = flag(iota((home, nb * WIN), 1) == source)

    def x_to_y(c):
        for d in farthest_first(nt):
            x_copy(c, d, True).wait_recv()
        if c + ahead < chunks:
            x_start(c + ahead)
        xrecv[c][tab_id] = xsend[c][tab_id]
        width = widths[c]
        out = dot_nn(smat[...], xrecv[c][...].reshape(nt * pair, width))
        for b in range(nb):
            block = out[b * MAXLEN : (b + 1) * MAXLEN]
            if width > 128:
                block = jnp.concatenate([block[:, : width // 2], block[:, width // 2 :]], axis=0)
            else:
                block = jnp.concatenate([block, jnp.zeros((WIN - MAXLEN, width), F32)], axis=0)
            ysend[c][b] = block.astype(BF16)
        for d in farthest_first(nb):
            y_copy(c, d).start()
        yrecv[c][bal_id] = ysend[c][bal_id]

    def y_in(c):
        width = widths[c]
        for d in farthest_first(nb):
            y_copy(c, d, True).wait_recv()
        if width > 128:
            for s in range(nb):
                block = yrecv[c][s].astype(F32)
                block = jnp.concatenate([block[:MAXLEN], block[MAXLEN:]], axis=1)
                block = jnp.concatenate([block, jnp.zeros((WIN - MAXLEN, width), F32)], axis=0)
                spread[s * WIN : (s + 1) * WIN, :width] = block.astype(BF16)
            arrived = spread[:, :width]
        else:
            arrived = yrecv[c][...].reshape(nb * WIN, width)
        bal[:, firsts[c] : firsts[c] + width] = dot_nn(tmat[...], arrived).astype(BF16)

    def turn_out_grad():
        loads[5].wait()
        for b in range(nb):
            cols = 16 * nt
            turned = og[:, b * cols : (b + 1) * cols].T
            ogp[:, b * 16 : (b + 1) * 16, :] = turned.reshape(nt, 16, home)
        for x in range(nx):
            o_copy(x).start()

    def mask_scale(in_off):
        query, key = iota((TILE, 2 * TILE), 0), iota((TILE, 2 * TILE), 1)
        for i in range(tiles):
            at = query + i * TILE
            source = key + (i - 1) * TILE
            first = jnp.zeros_like(at)
            for s in range(1, nb):
                first = jnp.where(in_off[s] <= at, in_off[s], first)
            scale[i] = jnp.where((source <= at) & (source >= first), 0.5 * HEAD**-0.5, 0.0)

    step = 1024
    early = firsts[-1]

    def project_early():
        loads[6].wait()

        @pl.loop(0, 4 * model // step)
        def _(n):
            cols = pl.ds(pl.multiple_of(n * step, step), step)
            acc[:, cols] = dot_nn(bal[:, :early], w[:early, cols])

    def project_late():
        @pl.loop(0, 4 * model // step)
        def _(n):
            cols = pl.ds(pl.multiple_of(n * step, step), step)
            half = 0.5 * (acc[:, cols] + dot_nn(bal[:, early:], w[early:, cols]))
            prj[:, cols] = (half + half * jnp.tanh(half)).astype(BF16)

    def attend(i):
        rows = slice(i * TILE, (i + 1) * TILE)
        low = max(0, i - 1) * TILE
        keys = slice(low, (i + 1) * TILE)
        lanes = slice(2 * TILE - (i + 1) * TILE + low, 2 * TILE)

        @pl.loop(0, heads // 8)
        def _(some):
            def cols(part, k):
                at = part * model + (some * 8 + k) * HEAD
                return pl.ds(pl.multiple_of(at, HEAD), HEAD)

            scores = [dot_nt(prj[rows, cols(2, k)], prj[keys, cols(3, k)]) for k in range(8)]
            halves = [part * scale[i, :, lanes] for part in scores]
            weights = [(half + half * jnp.tanh(half)).astype(BF16) for half in halves]
            for k in range(8):
                asum[rows, cols(0, k)] = dot_nn(weights[k], prj[keys, cols(1, k)])

    def gate(i):
        rows = slice(i * TILE, (i + 1) * TILE)
        att[rows, :] = (normalize(asum[rows, :]) * prj[rows, :model].astype(F32)).astype(BF16)

    def partial(x, cols):
        return dot_nn(ogp[2 * x + core], att[:, cols]) + dot_nn(ogr[x], attr[:, cols])

    def columns(g):
        return slice(gfirsts[g], gfirsts[g] + groups[g][1])

    def grad_start(g):
        axes, width, _ = groups[g]
        if axes == "xy":
            for d in farthest_first(nx) + [0]:
                x = lax.rem(x_id + d, nx)
                first_out[g][x] = partial(x, columns(g)).astype(BF16)
                if d:
                    first_copy(g, d).start()
        else:
            for x in range(nx):
                part = partial(x, columns(g)).astype(BF16)
                first_out[g][:, x * 16 : (x + 1) * 16, :] = part.reshape(nb, 16, width)
            for d in farthest_first(nb):
                first_copy(g, d).start()

    def gather(axis, copy, g, own, others):
        _, me, count = over(axis)
        total = own[g][me].astype(F32)
        for d in farthest_first(count)[::-1]:
            copy(g, d, True).wait_recv()
            total = total + others[g][lax.rem(me + d, count)].astype(F32)
        return total.astype(BF16)

    def grad_turn(g):
        axes, width, _ = groups[g]
        total = gather(axes[0], first_copy, g, first_out, first_in)
        _, _, count = over(axes[1])
        next_out[g][...] = total.reshape(count, 16, width)
        for d in farthest_first(count):
            next_copy(g, d).start()

    def grad_end(g):
        axes, width, whole = groups[g]
        total = gather(axes[1], next_copy, g, next_out, next_in)
        if whole:
            k = direct.index(g)
            whole_out[k][...] = total
            for d in farthest_first(nr):
                whole_copy(k, d).start()
            whole_in[k][rep_id] = total
        for j in range(nz):
            if owned[j][0] == g:
                at = owned[j][1] * TILE
                zs[j] = total[:, at : at + TILE]

                @pl.when(rep_id != j)
                def _():
                    z_copy(j).start()

    def grad_spread():
        @pl.when(rep_id < nz)
        def _():
            total = zs[rep_id].astype(F32)
            for d in range(1, nr):
                p = lax.rem(rep_id + d, nr)
                z_arrive(p).wait_recv()
                total = total + zr[p].astype(F32)
            zo[...] = total.astype(BF16)
            for d in farthest_first(nr):
                g_copy(d).start()
            zg[rep_id] = total.astype(BF16)

        for j in range(nz):

            @pl.when(rep_id != j)
            def _():
                g_arrive(j).wait_recv()

            at = gfirsts[owned[j][0]] + owned[j][1] * TILE
            grad_ref[:, at : at + TILE] = zg[j]
        for k, g in enumerate(direct):
            for d in range(1, nr):
                whole_copy(k, d, True).wait_recv()
            total = whole_in[k][0].astype(F32)
            for r in range(1, nr):
                total = total + whole_in[k][r].astype(F32)
            grad_ref[:, columns(g)] = total.astype(BF16)

    def all_sent():
        for c in range(chunks):
            for d in range(1, nt):
                x_copy(c, d).wait_send()
            for d in range(1, nb):
                y_copy(c, d).wait_send()
        for x in range(nx):
            o_copy(x).wait_send()
        for i in range(tiles):
            a_copy(i).wait_send()
        for g in range(gcount):
            for copy, axis in zip((first_copy, next_copy), groups[g][0]):
                for d in range(1, over(axis)[2]):
                    copy(g, d).wait_send()
        for k in range(len(direct)):
            for d in range(1, nr):
                whole_copy(k, d).wait_send()
        for j in range(nz):

            @pl.when(rep_id != j)
            def _():
                z_copy(j).wait_send()

        @pl.when(rep_id < nz)
        def _():
            for d in range(1, nr):
                g_copy(d).wait_send()

    load_and_greet()
    normalize_rows()
    greeted()
    hop_signal(0)
    for c in range(min(ahead, chunks)):
        x_start(c)
    start, length, in_off = history_bounds()
    placements(start, length, in_off)
    for c in range(chunks):
        x_to_y(c)
    turn_out_grad()
    mask_scale(in_off)
    for c in range(chunks - 1):
        y_in(c)
        if c < hops:
            hop_wait(c)
            if c + 1 < hops:
                hop_signal(c + 1)
    project_early()
    y_in(chunks - 1)
    project_late()
    for i in range(tiles):
        attend(i)
        gate(i)
        a_copy(i).start()
    att_copy.start()
    for x in range(nx):
        o_copy(x).wait_recv()
    for i in range(tiles):
        a_copy(i).wait_recv()
    for g in range(gcount):
        grad_start(g)
    for k in range(chunks - 1, hops):
        hop_wait(k)
        if k + 1 < hops:
            hop_signal(k + 1)
    for g in range(gcount):
        grad_turn(g)
    for g in range(gcount):
        grad_end(g)
    grad_spread()
    all_sent()
    att_copy.wait()


def on_device(sizes, hot_rows, cold_rows, row_source, lengths, destination, proj_weight, out_grad):
    nr, nb, nt = sizes
    home, model = out_grad.shape
    most = hot_rows.shape[0] // nt
    widths = (128, 256, 256, 256, 128)
    ahead = 2
    groups = (
        ("xy", 256, False), ("yx", 256, False), ("xy", 256, True), ("yx", 128, True),
        ("xy", 128, True),
    )
    chunks, gcount = len(widths), len(groups)
    nx, pair = nt // 2, 2 * most
    nz = sum(width // TILE for _, width, whole in groups if not whole)
    wholes = [width for _, width, whole in groups if whole]
    vmem = pltpu.VMEM
    dma = pltpu.SemaphoreType.DMA

    def y_block(width):
        return (2 * MAXLEN, width // 2) if width > 128 else (WIN, width)

    x_parts = [vmem((nt, pair, width), BF16) for width in widths]
    y_parts = [vmem((nb, *y_block(width)), BF16) for width in widths]
    def shares(axis, rows):
        return (nx, rows // nx) if axis == "x" else (nb, rows // nb)

    firsts = [vmem((*shares(axes[0], nx * nb * 16), width), BF16) for axes, width, _ in groups]
    nexts = [vmem((nx if axes[1] == "x" else nb, 16, width), BF16) for axes, width, _ in groups]
    scratch = [
        x_parts,
        x_parts,
        y_parts,
        y_parts,
        firsts,
        firsts,
        nexts,
        nexts,
        [vmem((16, width), BF16) for width in wholes],
        [vmem((nr, 16, width), BF16) for width in wholes],
        vmem((1, home), jnp.int32),
        pltpu.SMEM(lengths.shape, jnp.int32),
        pltpu.SMEM(destination.shape, jnp.int32),
        vmem(hot_rows.shape, F32),
        vmem(cold_rows.shape, BF16),
        vmem(proj_weight.shape, BF16),
        vmem(out_grad.shape, BF16),
        vmem((nt, nb * 16, home), BF16),
        vmem((nx, nb * 16, home), BF16),
        vmem((nt * pair, home), BF16),
        vmem((nb * MAXLEN, nt * pair), BF16),
        vmem((nb * WIN, max(widths)), BF16),
        vmem((home, nb * WIN), BF16),
        vmem((home, model), BF16),
        vmem((home, 4 * model), F32),
        vmem((home, 4 * model), BF16),
        vmem((home // TILE, TILE, 2 * TILE), F32),
        vmem((home, model), F32),
        vmem((home, model), BF16),
        vmem((home, model), BF16),
        vmem((nz, 16, TILE), BF16),
        vmem((nr, 16, TILE), BF16),
        vmem((16, TILE), BF16),
        vmem((nz, 16, TILE), BF16),
        dma((8,)),
        dma((chunks, nt)),
        dma((chunks, nt)),
        dma((chunks, nb)),
        dma((chunks, nb)),
        dma((nx,)),
        dma((nx,)),
        dma((home // TILE,)),
        dma((home // TILE,)),
        dma((gcount, max(nx, nb))),
        dma((gcount, max(nx, nb))),
        dma((gcount, max(nx, nb))),
        dma((gcount, max(nx, nb))),
        dma((len(wholes), nr)),
        dma((len(wholes), nr)),
        dma((nz,)),
        dma((nr,)),
        dma((nr,)),
        dma((nz,)),
        pltpu.SemaphoreType.REGULAR((nr // 2 - 1, 2)),
    ]
    hbm = pl.BlockSpec(memory_space=pl.ANY)
    return pl.pallas_call(
        functools.partial(layer_kernel, nr, nb, nt, most, widths, ahead, groups),
        out_shape=(
            jax.ShapeDtypeStruct((home, model), BF16),
            jax.ShapeDtypeStruct((model // (nb * nt), model), BF16),
        ),
        in_specs=[hbm] * 7,
        out_specs=(hbm, pl.BlockSpec(memory_space=pltpu.VMEM)),
        scratch_shapes=scratch,
        compiler_params=pltpu.CompilerParams(
            collective_id=0, has_side_effects=True, vmem_limit_bytes=58 * 1024 * 1024
        ),
    )(
        hot_rows,
        cold_rows,
        row_source.reshape(1, home),
        lengths,
        destination,
        proj_weight,
        out_grad,
    )


def solution(mesh):
    sizes = tuple(mesh.shape[axis] for axis in ("rep", "bal", "tab"))
    in_specs = (
        P(("rep", "bal", "tab"), None),
        P(("rep", "bal", "tab"), None),
        P(("rep", "bal", "tab"), None),
        P("rep", None, "tab", None),
        P("rep", None, "tab", None),
        P(),
        P(("rep", "bal", "tab"), None),
    )
    out_specs = (P(("rep", "bal", "tab"), None), P(("bal", "tab"), None))
    return jax.shard_map(
        functools.partial(on_device, sizes),
        mesh=mesh,
        in_specs=in_specs,
        out_specs=out_specs,
        check_vma=False,
    )
```

```python
import functools

import jax
import jax.numpy as jnp
from jax import lax
from jax.experimental import pallas as pl
from jax.experimental.pallas import tpu as pltpu
from jax.sharding import PartitionSpec as P

HEAD = 128
MAXLEN = 88
WIN = 96
F32, BF16 = jnp.float32, jnp.bfloat16
TILE = 128


def iota(shape, dim):
    return lax.broadcasted_iota(jnp.int32, shape, dim)


def normalize(rows_in):
    center = jnp.mean(rows_in, axis=-1, keepdims=True)
    centered = rows_in - center
    deviation = jnp.mean(centered * centered, axis=-1, keepdims=True)
    return centered * lax.rsqrt(deviation + 1e-05)


def dot_nt(a, b):
    return lax.dot_general(a, b, (((1,), (1,)), ((), ())), preferred_element_type=F32)


def dot_nn(a, b):
    return jnp.dot(a, b, preferred_element_type=F32)


def flag(cond):
    return jnp.where(cond, 1.0, 0.0).astype(BF16)


def farthest_first(count):
    return sorted(range(1, count), key=lambda d: -min(d, count - d))


def layer_kernel(
    nr, nb, nt, most, widths, ahead, groups,
    hot_hbm, cold_hbm, code_hbm, len_hbm, dest_hbm, w_hbm, og_hbm,
    att_hbm, grad_ref,
    xsend, xrecv, ysend, yrecv, first_out, first_in, next_out, next_in, whole_out, whole_in, gown,
    code_ref, len_ref, dest_ref,
    hot, cold, w, og, ogp, ogr, bmat, smat, spread, tmat, bal, acc, prj, scale,
    asum, att, attr, zs, zr, zo, zg,
    load_sem, row_sem, xs_sem, xr_sem, ys_sem, yr_sem, os_sem, or_sem, as_sem, ar_sem,
    fs_sem, fr_sem, ns_sem, nr_sem, ws_sem, wr_sem, zs_sem, zr_sem, gs_sem, gr_sem, hop_sem,
):
    home, model = og.shape
    nx = nt // 2
    chunks = len(widths)
    firsts = [sum(widths[:c]) for c in range(chunks)]
    tiles = home // TILE
    heads = model // HEAD
    pair = 2 * most
    gcount = len(groups)
    gfirsts = [sum(width for _, width, _ in groups[:g]) for g in range(gcount)]
    direct = [g for g in range(gcount) if groups[g][2]]
    owned = [
        (g, k) for g in range(gcount) if not groups[g][2] for k in range(groups[g][1] // TILE)
    ]
    nz = len(owned)
    rep_id = lax.axis_index("rep")
    bal_id = lax.axis_index("bal")
    tab_id = lax.axis_index("tab")
    core = lax.rem(tab_id, 2)
    x_id = lax.div(tab_id, 2)
    sibling = tab_id + 1 - 2 * core

    loads = [
        pltpu.make_async_copy(src, dst, load_sem.at[i])
        for i, (src, dst) in enumerate(
            (
                (code_hbm, code_ref), (len_hbm, len_ref), (dest_hbm, dest_ref), (og_hbm, og),
                (w_hbm, w),
            )
        )
    ]
    att_copy = pltpu.make_async_copy(att, att_hbm, load_sem.at[5])

    def row_loads(i):
        rows = pl.ds(pl.multiple_of(i * 2 * most, 16), 2 * most)
        return [
            pltpu.make_async_copy(src.at[rows], dst.at[rows], row_sem.at[k, i])
            for k, (src, dst) in enumerate(((hot_hbm, hot), (cold_hbm, cold)))
        ]

    def remote(src, dst, send, recv, axis, peer):
        return pltpu.make_async_remote_copy(
            src_ref=src, dst_ref=dst, send_sem=send, recv_sem=recv, device_id={axis: peer}
        )

    def exchange(src, dst, send, recv, axis, me, count, d, c, arriving):
        p = lax.rem(me + d, count)
        at = p if arriving else me
        peer = 2 * p + core if axis == "x" else p
        return remote(
            src.at[p], dst.at[at], send.at[c, p], recv.at[c, at], "tab" if axis == "x" else axis, peer
        )

    def x_copy(c, d, arriving=False):
        return exchange(xsend[c], xrecv[c], xs_sem, xr_sem, "tab", tab_id, nt, d, c, arriving)

    def y_copy(c, d, arriving=False):
        return exchange(ysend[c], yrecv[c], ys_sem, yr_sem, "bal", bal_id, nb, d, c, arriving)

    def over(axis):
        return ("x", x_id, nx) if axis == "x" else ("bal", bal_id, nb)

    def first_copy(g, d, arriving=False):
        axis = over(groups[g][0][0])
        return exchange(first_out[g], first_in[g], fs_sem, fr_sem, *axis, d, g, arriving)

    def next_copy(g, d, arriving=False):
        axis = over(groups[g][0][1])
        return exchange(next_out[g], next_in[g], ns_sem, nr_sem, *axis, d, g, arriving)

    def whole_copy(k, d, arriving=False):
        p = lax.rem(rep_id + d, nr)
        at = p if arriving else rep_id
        return remote(
            whole_out[k], whole_in[k].at[at], ws_sem.at[k, p], wr_sem.at[k, at], "rep", p
        )

    def o_copy(x):
        return remote(
            ogp.at[2 * x + 1 - core], ogr.at[x], os_sem.at[x], or_sem.at[x], "tab", sibling
        )

    def a_copy(i):
        rows = pl.ds(i * TILE, TILE)
        return remote(att.at[rows], attr.at[rows], as_sem.at[i], ar_sem.at[i], "tab", sibling)

    def z_copy(j):
        return remote(zs.at[j], zr.at[rep_id], zs_sem.at[j], zr_sem.at[rep_id], "rep", j)

    def z_arrive(p):
        return remote(zs.at[0], zr.at[p], zs_sem.at[0], zr_sem.at[p], "rep", p)

    def g_copy(d):
        p = lax.rem(rep_id + d, nr)
        return remote(zo, zg.at[rep_id], gs_sem.at[p], gr_sem.at[rep_id], "rep", p)

    def g_arrive(j):
        return remote(zo, zg.at[j], gs_sem.at[0], gr_sem.at[j], "rep", j)

    def load_and_greet():
        for i in range(nx):
            for load in row_loads(i):
                load.start()
        for load in loads[:3]:
            load.start()
        barrier = pltpu.get_barrier_semaphore()
        for axis, me, count, reach in (
            ("tab", tab_id, nt, range(1, nt)),
            ("bal", bal_id, nb, range(1, nb)),
            ("rep", rep_id, nr, (1, nr - 1)),
        ):
            for d in reach:
                pl.semaphore_signal(barrier, inc=1, device_id={axis: lax.rem(me + d, count)})

    def normalize_rows():
        @pl.loop(0, nx)
        def _(i):
            rows = pl.ds(pl.multiple_of(i * 2 * most, 16), 2 * most)
            for load in row_loads(i):
                load.wait()
            hot_n = normalize(hot[rows, :])
            cold_n = normalize(cold[rows, :].astype(F32))
            for k in range(2):
                part = slice(k * most, (k + 1) * most)
                block = jnp.concatenate([hot_n[part], cold_n[part]], axis=0).astype(BF16)
                for c in range(chunks):
                    xsend[c][2 * i + k] = block[:, firsts[c] : firsts[c] + widths[c]]

    def greeted():
        for load in loads[3:]:
            load.start()
        pl.semaphore_wait(pltpu.get_barrier_semaphore(), nt - 1 + nb - 1 + 2)

    hops = nr // 2 - 1

    def hop_signal(k):
        for side in range(2):
            peer = lax.rem(rep_id + (nr - 1 if side else 1), nr)
            pl.semaphore_signal(hop_sem.at[k, side], inc=1, device_id={"rep": peer})

    def hop_wait(k):
        for side in range(2):
            pl.semaphore_wait(hop_sem.at[k, side], 1)

    def x_start(c):
        for d in farthest_first(nt):
            x_copy(c, d).start()

    def history_bounds():
        for load in loads[:3]:
            load.wait()
        start = [jnp.int32(0)] * nb
        length = [jnp.int32(0)] * nb
        run = jnp.int32(0)
        for h in range(nb):
            here = len_ref[0, bal_id, 0, h]
            goal = dest_ref[0, bal_id, 0, h]
            for b in range(nb):
                start[b] = jnp.where(goal == b, run, start[b])
                length[b] = jnp.where(goal == b, here, length[b])
            run = run + here
        in_off = []
        run = jnp.int32(0)
        for s in range(nb):
            in_off.append(run)
            for h in range(nb):
                run = run + jnp.where(dest_ref[0, s, 0, h] == bal_id, len_ref[0, s, 0, h], 0)
        return start, length, in_off

    def placements(start, length, in_off):
        codes = code_ref[...]
        flags = jnp.where(iota((2 * nt, home), 0) == codes, 1.0, 0.0)
        before = flag(iota((home, home), 0) < iota((home, home), 1))
        earlier = dot_nn(flags.astype(BF16), before)
        slot = jnp.sum(flags * earlier, axis=0, keepdims=True).astype(jnp.int32)
        tier = jnp.where(codes >= nt, 1, 0)
        place = (codes - nt * tier) * pair + tier * most + slot
        bmat[...] = flag(iota((nt * pair, home), 0) == place)
        gap = iota((MAXLEN, home), 1) - iota((MAXLEN, home), 0)
        offset = iota((MAXLEN, home), 0)
        for b in range(0, nb, 2):
            chosen = jnp.concatenate(
                [
                    jnp.where((gap == start[k]) & (offset < length[k]), 1.0, 0.0)
                    for k in (b, b + 1)
                ],
                axis=0,
            ).astype(BF16)
            smat[b * MAXLEN : (b + 2) * MAXLEN, :] = dot_nt(chosen, bmat[...]).astype(BF16)
        row = iota((home, WIN), 0)
        moved = jnp.zeros_like(row)
        for s in range(1, nb):
            moved = jnp.where(row >= in_off[s], s * WIN - in_off[s], moved)
        source = (row + moved)[:, :1]
        tmat[...] = flag(iota((home, nb * WIN), 1) == source)

    def x_to_y(c):
        for d in farthest_first(nt):
            x_copy(c, d, True).wait_recv()
        if c + ahead < chunks:
            x_start(c + ahead)
        xrecv[c][tab_id] = xsend[c][tab_id]
        width = widths[c]
        out = dot_nn(smat[...], xrecv[c][...].reshape(nt * pair, width))
        for b in range(nb):
            block = out[b * MAXLEN : (b + 1) * MAXLEN]
            if width > 128:
                block = jnp.concatenate([block[:, : width // 2], block[:, width // 2 :]], axis=0)
            else:
                block = jnp.concatenate([block, jnp.zeros((WIN - MAXLEN, width), F32)], axis=0)
            ysend[c][b] = block.astype(BF16)
        for d in farthest_first(nb):
            y_copy(c, d).start()
        yrecv[c][bal_id] = ysend[c][bal_id]

    def y_in(c):
        width = widths[c]
        for d in farthest_first(nb):
            y_copy(c, d, True).wait_recv()
        if width > 128:
            for s in range(nb):
                block = yrecv[c][s].astype(F32)
                block = jnp.concatenate([block[:MAXLEN], block[MAXLEN:]], axis=1)
                block = jnp.concatenate([block, jnp.zeros((WIN - MAXLEN, width), F32)], axis=0)
                spread[s * WIN : (s + 1) * WIN, :width] = block.astype(BF16)
            arrived = spread[:, :width]
        else:
            arrived = yrecv[c][...].reshape(nb * WIN, width)
        bal[:, firsts[c] : firsts[c] + width] = dot_nn(tmat[...], arrived).astype(BF16)

    def turn_out_grad():
        loads[3].wait()
        for b in range(nb):
            cols = 16 * nt
            turned = og[:, b * cols : (b + 1) * cols].T
            ogp[:, b * 16 : (b + 1) * 16, :] = turned.reshape(nt, 16, home)
        for x in range(nx):
            o_copy(x).start()

    def mask_scale(in_off):
        query, key = iota((TILE, 2 * TILE), 0), iota((TILE, 2 * TILE), 1)
        for i in range(tiles):
            at = query + i * TILE
            source = key + (i - 1) * TILE
            first = jnp.zeros_like(at)
            for s in range(1, nb):
                first = jnp.where(in_off[s] <= at, in_off[s], first)
            scale[i] = jnp.where((source <= at) & (source >= first), 0.5 * HEAD**-0.5, 0.0)

    step = 1024
    early = firsts[-2]

    def project_early():
        loads[4].wait()

        @pl.loop(0, 4 * model // step)
        def _(n):
            cols = pl.ds(pl.multiple_of(n * step, step), step)
            acc[:, cols] = dot_nn(bal[:, :early], w[:early, cols])

    def project_late():
        @pl.loop(0, 4 * model // step)
        def _(n):
            cols = pl.ds(pl.multiple_of(n * step, step), step)
            half = 0.5 * (acc[:, cols] + dot_nn(bal[:, early:], w[early:, cols]))
            prj[:, cols] = (half + half * jnp.tanh(half)).astype(BF16)

    def attend(i):
        rows = slice(i * TILE, (i + 1) * TILE)
        low = max(0, i - 1) * TILE
        keys = slice(low, (i + 1) * TILE)
        lanes = slice(2 * TILE - (i + 1) * TILE + low, 2 * TILE)

        @pl.loop(0, heads // 8)
        def _(some):
            def cols(part, k):
                at = part * model + (some * 8 + k) * HEAD
                return pl.ds(pl.multiple_of(at, HEAD), HEAD)

            scores = [dot_nt(prj[rows, cols(2, k)], prj[keys, cols(3, k)]) for k in range(8)]
            halves = [part * scale[i, :, lanes] for part in scores]
            weights = [(half + half * jnp.tanh(half)).astype(BF16) for half in halves]
            for k in range(8):
                asum[rows, cols(0, k)] = dot_nn(weights[k], prj[keys, cols(1, k)])

    def gate(i):
        rows = slice(i * TILE, (i + 1) * TILE)
        att[rows, :] = (normalize(asum[rows, :]) * prj[rows, :model].astype(F32)).astype(BF16)

    def partial_own(g):
        for x in range(nx):
            gown[g][x] = dot_nn(ogp[2 * x + core], att[:, columns(g)])

    def partial(g, x):
        if g < len(gown):
            own = gown[g][x]
        else:
            own = dot_nn(ogp[2 * x + core], att[:, columns(g)])
        return own + dot_nn(ogr[x], attr[:, columns(g)])

    def columns(g):
        return slice(gfirsts[g], gfirsts[g] + groups[g][1])

    def grad_start(g):
        axes, width, _ = groups[g]
        if axes == "xy":
            for d in farthest_first(nx) + [0]:
                x = lax.rem(x_id + d, nx)
                first_out[g][x] = partial(g, x).astype(BF16)
                if d:
                    first_copy(g, d).start()
        else:
            for x in range(nx):
                part = partial(g, x).astype(BF16)
                first_out[g][:, x * 16 : (x + 1) * 16, :] = part.reshape(nb, 16, width)
            for d in farthest_first(nb):
                first_copy(g, d).start()

    def gather(axis, copy, g, own, others):
        _, me, count = over(axis)
        total = own[g][me].astype(F32)
        for d in farthest_first(count)[::-1]:
            copy(g, d, True).wait_recv()
            total = total + others[g][lax.rem(me + d, count)].astype(F32)
        return total.astype(BF16)

    def grad_turn(g):
        axes, width, _ = groups[g]
        total = gather(axes[0], first_copy, g, first_out, first_in)
        _, _, count = over(axes[1])
        next_out[g][...] = total.reshape(count, 16, width)
        for d in farthest_first(count):
            next_copy(g, d).start()

    def grad_end(g):
        axes, width, whole = groups[g]
        total = gather(axes[1], next_copy, g, next_out, next_in)
        if whole:
            k = direct.index(g)
            whole_out[k][...] = total
            for d in farthest_first(nr):
                whole_copy(k, d).start()
            whole_in[k][rep_id] = total
        for j in range(nz):
            if owned[j][0] == g:
                at = owned[j][1] * TILE
                zs[j] = total[:, at : at + TILE]

                @pl.when(rep_id != j)
                def _():
                    z_copy(j).start()

    def grad_spread():
        @pl.when(rep_id < nz)
        def _():
            total = zs[rep_id].astype(F32)
            for d in range(1, nr):
                p = lax.rem(rep_id + d, nr)
                z_arrive(p).wait_recv()
                total = total + zr[p].astype(F32)
            zo[...] = total.astype(BF16)
            for d in farthest_first(nr):
                g_copy(d).start()
            zg[rep_id] = total.astype(BF16)

        for j in range(nz):

            @pl.when(rep_id != j)
            def _():
                g_arrive(j).wait_recv()

            at = gfirsts[owned[j][0]] + owned[j][1] * TILE
            grad_ref[:, at : at + TILE] = zg[j]
        for k, g in enumerate(direct):
            for d in range(1, nr):
                whole_copy(k, d, True).wait_recv()
            total = whole_in[k][0].astype(F32)
            for r in range(1, nr):
                total = total + whole_in[k][r].astype(F32)
            grad_ref[:, columns(g)] = total.astype(BF16)

    def all_sent():
        for c in range(chunks):
            for d in range(1, nt):
                x_copy(c, d).wait_send()
            for d in range(1, nb):
                y_copy(c, d).wait_send()
        for x in range(nx):
            o_copy(x).wait_send()
        for i in range(tiles):
            a_copy(i).wait_send()
        for g in range(gcount):
            for copy, axis in zip((first_copy, next_copy), groups[g][0]):
                for d in range(1, over(axis)[2]):
                    copy(g, d).wait_send()
        for k in range(len(direct)):
            for d in range(1, nr):
                whole_copy(k, d).wait_send()
        for j in range(nz):

            @pl.when(rep_id != j)
            def _():
                z_copy(j).wait_send()

        @pl.when(rep_id < nz)
        def _():
            for d in range(1, nr):
                g_copy(d).wait_send()

    load_and_greet()
    normalize_rows()
    greeted()
    hop_signal(0)
    for c in range(min(ahead, chunks)):
        x_start(c)
    start, length, in_off = history_bounds()
    placements(start, length, in_off)
    for c in range(chunks):
        x_to_y(c)
    turn_out_grad()
    mask_scale(in_off)
    for c in range(chunks - 1):
        y_in(c)
        if c < hops:
            hop_wait(c)
            if c + 1 < hops:
                hop_signal(c + 1)
        if c == chunks - 3:
            project_early()
    y_in(chunks - 1)
    project_late()
    for i in range(tiles):
        attend(i)
        gate(i)
        a_copy(i).start()
    att_copy.start()
    for g in range(len(gown)):
        partial_own(g)
    for x in range(nx):
        o_copy(x).wait_recv()
    for i in range(tiles):
        a_copy(i).wait_recv()
    for g in range(gcount):
        grad_start(g)
    for k in range(chunks - 1, hops):
        hop_wait(k)
        if k + 1 < hops:
            hop_signal(k + 1)
    for g in range(gcount):
        grad_turn(g)
    for g in range(gcount):
        grad_end(g)
    grad_spread()
    all_sent()
    att_copy.wait()


def hand_over(att_in, grad_in, att_out, grad_out):
    att_out[...] = att_in[...]
    grad_out[...] = grad_in[...]


def on_device(sizes, hot_rows, cold_rows, row_source, lengths, destination, proj_weight, out_grad):
    nr, nb, nt = sizes
    home, model = out_grad.shape
    most = hot_rows.shape[0] // nt
    widths = (128, 256, 256, 256, 128)
    ahead = 2
    groups = (
        ("xy", 256, False), ("yx", 256, False), ("xy", 256, True), ("yx", 128, True),
        ("xy", 128, True),
    )
    chunks, gcount = len(widths), len(groups)
    nx, pair = nt // 2, 2 * most
    nz = sum(width // TILE for _, width, whole in groups if not whole)
    wholes = [width for _, width, whole in groups if whole]
    vmem = pltpu.VMEM
    dma = pltpu.SemaphoreType.DMA

    def y_block(width):
        return (2 * MAXLEN, width // 2) if width > 128 else (WIN, width)

    x_parts = [vmem((nt, pair, width), BF16) for width in widths]
    y_parts = [vmem((nb, *y_block(width)), BF16) for width in widths]
    def shares(axis, rows):
        return (nx, rows // nx) if axis == "x" else (nb, rows // nb)

    firsts = [vmem((*shares(axes[0], nx * nb * 16), width), BF16) for axes, width, _ in groups]
    nexts = [vmem((nx if axes[1] == "x" else nb, 16, width), BF16) for axes, width, _ in groups]
    scratch = [
        x_parts,
        x_parts,
        y_parts,
        y_parts,
        firsts,
        firsts,
        nexts,
        nexts,
        [vmem((16, width), BF16) for width in wholes],
        [vmem((nr, 16, width), BF16) for width in wholes],
        [vmem((nx, nb * 16, width), F32) for _, width, _ in groups[:2]],
        vmem((1, home), jnp.int32),
        pltpu.SMEM(lengths.shape, jnp.int32),
        pltpu.SMEM(destination.shape, jnp.int32),
        vmem(hot_rows.shape, F32),
        vmem(cold_rows.shape, BF16),
        vmem(proj_weight.shape, BF16),
        vmem(out_grad.shape, BF16),
        vmem((nt, nb * 16, home), BF16),
        vmem((nx, nb * 16, home), BF16),
        vmem((nt * pair, home), BF16),
        vmem((nb * MAXLEN, nt * pair), BF16),
        vmem((nb * WIN, max(widths)), BF16),
        vmem((home, nb * WIN), BF16),
        vmem((home, model), BF16),
        vmem((home, 4 * model), F32),
        vmem((home, 4 * model), BF16),
        vmem((home // TILE, TILE, 2 * TILE), F32),
        vmem((home, model), F32),
        vmem((home, model), BF16),
        vmem((home, model), BF16),
        vmem((nz, 16, TILE), BF16),
        vmem((nr, 16, TILE), BF16),
        vmem((16, TILE), BF16),
        vmem((nz, 16, TILE), BF16),
        dma((6,)),
        dma((2, nx)),
        dma((chunks, nt)),
        dma((chunks, nt)),
        dma((chunks, nb)),
        dma((chunks, nb)),
        dma((nx,)),
        dma((nx,)),
        dma((home // TILE,)),
        dma((home // TILE,)),
        dma((gcount, max(nx, nb))),
        dma((gcount, max(nx, nb))),
        dma((gcount, max(nx, nb))),
        dma((gcount, max(nx, nb))),
        dma((len(wholes), nr)),
        dma((len(wholes), nr)),
        dma((nz,)),
        dma((nr,)),
        dma((nr,)),
        dma((nz,)),
        pltpu.SemaphoreType.REGULAR((nr // 2 - 1, 2)),
    ]
    hbm = pl.BlockSpec(memory_space=pl.ANY)
    att, grad = pl.pallas_call(
        functools.partial(layer_kernel, nr, nb, nt, most, widths, ahead, groups),
        out_shape=(
            jax.ShapeDtypeStruct((home, model), BF16),
            jax.ShapeDtypeStruct((model // (nb * nt), model), BF16),
        ),
        in_specs=[hbm] * 7,
        out_specs=(hbm, pl.BlockSpec(memory_space=pltpu.VMEM)),
        scratch_shapes=scratch,
        compiler_params=pltpu.CompilerParams(
            collective_id=0, has_side_effects=True, vmem_limit_bytes=58 * 1024 * 1024
        ),
    )(
        hot_rows,
        cold_rows,
        row_source.reshape(1, home),
        lengths,
        destination,
        proj_weight,
        out_grad,
    )
    parts = 3
    return pl.pallas_call(
        hand_over,
        grid=(parts,),
        out_shape=(
            jax.ShapeDtypeStruct(att.shape, att.dtype),
            jax.ShapeDtypeStruct(grad.shape, grad.dtype),
        ),
        in_specs=[
            pl.BlockSpec((home // parts, model), lambda i: (i, 0)),
            pl.BlockSpec(grad.shape, lambda i: (0, 0)),
        ],
        out_specs=(
            pl.BlockSpec((home // parts, model), lambda i: (i, 0)),
            pl.BlockSpec(grad.shape, lambda i: (0, 0)),
        ),
    )(att, grad)


def solution(mesh):
    sizes = tuple(mesh.shape[axis] for axis in ("rep", "bal", "tab"))
    in_specs = (
        P(("rep", "bal", "tab"), None),
        P(("rep", "bal", "tab"), None),
        P(("rep", "bal", "tab"), None),
        P("rep", None, "tab", None),
        P("rep", None, "tab", None),
        P(),
        P(("rep", "bal", "tab"), None),
    )
    out_specs = (P(("rep", "bal", "tab"), None), P(("bal", "tab"), None))
    return jax.shard_map(
        functools.partial(on_device, sizes),
        mesh=mesh,
        in_specs=in_specs,
        out_specs=out_specs,
        check_vma=False,
    )
```

```python
import functools

import jax
import jax.numpy as jnp
from jax import lax
from jax.experimental import pallas as pl
from jax.experimental.pallas import tpu as pltpu
from jax.sharding import PartitionSpec as P

HEAD = 128
MAXLEN = 88
WIN = 96
F32, BF16 = jnp.float32, jnp.bfloat16
TILE = 128


def iota(shape, dim):
    return lax.broadcasted_iota(jnp.int32, shape, dim)


def normalize(rows_in):
    center = jnp.mean(rows_in, axis=-1, keepdims=True)
    centered = rows_in - center
    deviation = jnp.mean(centered * centered, axis=-1, keepdims=True)
    return centered * lax.rsqrt(deviation + 1e-05)


def dot_nt(a, b):
    return lax.dot_general(a, b, (((1,), (1,)), ((), ())), preferred_element_type=F32)


def dot_nn(a, b):
    return jnp.dot(a, b, preferred_element_type=F32)


def flag(cond):
    return jnp.where(cond, 1.0, 0.0).astype(BF16)


def farthest_first(count):
    return sorted(range(1, count), key=lambda d: -min(d, count - d))


def layer_kernel(
    nr, nb, nt, most, widths, ahead, groups,
    hot_hbm, cold_hbm, code_hbm, len_hbm, dest_hbm, w_hbm, og_hbm,
    att_hbm, grad_ref,
    xsend, xrecv, ysend, yrecv, first_out, first_in, next_out, next_in, whole_out, whole_in, gown,
    code_ref, len_ref, dest_ref,
    hot, cold, w, og, ogp, ogr, bmat, smat, spread, tmat, bal, acc, prj, scale,
    asum, att, attr, zs, zr, zo, zg,
    load_sem, row_sem, xs_sem, xr_sem, ys_sem, yr_sem, os_sem, or_sem, as_sem, ar_sem,
    fs_sem, fr_sem, ns_sem, nr_sem, ws_sem, wr_sem, zs_sem, zr_sem, gs_sem, gr_sem, hop_sem,
):
    home, model = og.shape
    nx = nt // 2
    chunks = len(widths)
    firsts = [sum(widths[:c]) for c in range(chunks)]
    tiles = home // TILE
    heads = model // HEAD
    pair = 2 * most
    gcount = len(groups)
    gfirsts = [sum(width for _, width, _ in groups[:g]) for g in range(gcount)]
    direct = [g for g in range(gcount) if groups[g][2]]
    owned = [
        (g, k) for g in range(gcount) if not groups[g][2] for k in range(groups[g][1] // TILE)
    ]
    nz = len(owned)
    rep_id = lax.axis_index("rep")
    bal_id = lax.axis_index("bal")
    tab_id = lax.axis_index("tab")
    core = lax.rem(tab_id, 2)
    x_id = lax.div(tab_id, 2)
    sibling = tab_id + 1 - 2 * core

    loads = [
        pltpu.make_async_copy(src, dst, load_sem.at[i])
        for i, (src, dst) in enumerate(
            (
                (code_hbm, code_ref), (len_hbm, len_ref), (dest_hbm, dest_ref), (og_hbm, og),
                (w_hbm, w),
            )
        )
    ]
    att_copy = pltpu.make_async_copy(att, att_hbm, load_sem.at[5])

    def row_loads(i):
        rows = pl.ds(pl.multiple_of(i * 2 * most, 16), 2 * most)
        return [
            pltpu.make_async_copy(src.at[rows], dst.at[rows], row_sem.at[k, i])
            for k, (src, dst) in enumerate(((hot_hbm, hot), (cold_hbm, cold)))
        ]

    def remote(src, dst, send, recv, axis, peer):
        return pltpu.make_async_remote_copy(
            src_ref=src, dst_ref=dst, send_sem=send, recv_sem=recv, device_id={axis: peer}
        )

    def exchange(src, dst, send, recv, axis, me, count, d, c, arriving):
        p = lax.rem(me + d, count)
        at = p if arriving else me
        peer = 2 * p + core if axis == "x" else p
        return remote(
            src.at[p], dst.at[at], send.at[c, p], recv.at[c, at], "tab" if axis == "x" else axis, peer
        )

    def x_copy(c, d, arriving=False):
        return exchange(xsend[c], xrecv[c], xs_sem, xr_sem, "tab", tab_id, nt, d, c, arriving)

    def y_copy(c, d, arriving=False):
        return exchange(ysend[c], yrecv[c], ys_sem, yr_sem, "bal", bal_id, nb, d, c, arriving)

    def over(axis):
        return ("x", x_id, nx) if axis == "x" else ("bal", bal_id, nb)

    def first_copy(g, d, arriving=False):
        axis = over(groups[g][0][0])
        return exchange(first_out[g], first_in[g], fs_sem, fr_sem, *axis, d, g, arriving)

    def next_copy(g, d, arriving=False):
        axis = over(groups[g][0][1])
        return exchange(next_out[g], next_in[g], ns_sem, nr_sem, *axis, d, g, arriving)

    def whole_copy(k, d, arriving=False):
        p = lax.rem(rep_id + d, nr)
        at = p if arriving else rep_id
        return remote(
            whole_out[k], whole_in[k].at[at], ws_sem.at[k, p], wr_sem.at[k, at], "rep", p
        )

    def o_copy(x):
        return remote(
            ogp.at[2 * x + 1 - core], ogr.at[x], os_sem.at[x], or_sem.at[x], "tab", sibling
        )

    def a_copy(i):
        rows = pl.ds(i * TILE, TILE)
        return remote(att.at[rows], attr.at[rows], as_sem.at[i], ar_sem.at[i], "tab", sibling)

    def z_copy(j):
        return remote(zs.at[j], zr.at[rep_id], zs_sem.at[j], zr_sem.at[rep_id], "rep", j)

    def z_arrive(p):
        return remote(zs.at[0], zr.at[p], zs_sem.at[0], zr_sem.at[p], "rep", p)

    def g_copy(d):
        p = lax.rem(rep_id + d, nr)
        return remote(zo, zg.at[rep_id], gs_sem.at[p], gr_sem.at[rep_id], "rep", p)

    def g_arrive(j):
        return remote(zo, zg.at[j], gs_sem.at[0], gr_sem.at[j], "rep", j)

    def load_and_greet():
        for i in range(nx):
            for load in row_loads(i):
                load.start()
        for load in loads[:3]:
            load.start()
        barrier = pltpu.get_barrier_semaphore()
        for axis, me, count, reach in (
            ("tab", tab_id, nt, range(1, nt)),
            ("bal", bal_id, nb, range(1, nb)),
            ("rep", rep_id, nr, (1, nr - 1)),
        ):
            for d in reach:
                pl.semaphore_signal(barrier, inc=1, device_id={axis: lax.rem(me + d, count)})

    def normalize_rows():
        @pl.loop(0, nx)
        def _(i):
            rows = pl.ds(pl.multiple_of(i * 2 * most, 16), 2 * most)
            for load in row_loads(i):
                load.wait()
            hot_n = normalize(hot[rows, :])
            cold_n = normalize(cold[rows, :].astype(F32))
            for k in range(2):
                part = slice(k * most, (k + 1) * most)
                block = jnp.concatenate([hot_n[part], cold_n[part]], axis=0).astype(BF16)
                for c in range(chunks):
                    xsend[c][2 * i + k] = block[:, firsts[c] : firsts[c] + widths[c]]

    def greeted():
        for load in loads[3:]:
            load.start()
        pl.semaphore_wait(pltpu.get_barrier_semaphore(), nt - 1 + nb - 1 + 2)

    hops = nr // 2 - 1

    def hop_signal(k):
        for side in range(2):
            peer = lax.rem(rep_id + (nr - 1 if side else 1), nr)
            pl.semaphore_signal(hop_sem.at[k, side], inc=1, device_id={"rep": peer})

    def hop_wait(k):
        for side in range(2):
            pl.semaphore_wait(hop_sem.at[k, side], 1)

    def x_start(c):
        for d in farthest_first(nt):
            x_copy(c, d).start()

    def history_bounds():
        for load in loads[:3]:
            load.wait()
        start = [jnp.int32(0)] * nb
        length = [jnp.int32(0)] * nb
        run = jnp.int32(0)
        for h in range(nb):
            here = len_ref[0, bal_id, 0, h]
            goal = dest_ref[0, bal_id, 0, h]
            for b in range(nb):
                start[b] = jnp.where(goal == b, run, start[b])
                length[b] = jnp.where(goal == b, here, length[b])
            run = run + here
        in_off = []
        run = jnp.int32(0)
        for s in range(nb):
            in_off.append(run)
            for h in range(nb):
                run = run + jnp.where(dest_ref[0, s, 0, h] == bal_id, len_ref[0, s, 0, h], 0)
        return start, length, in_off

    def placements(start, length, in_off):
        codes = code_ref[...]
        flags = jnp.where(iota((2 * nt, home), 0) == codes, 1.0, 0.0)
        before = flag(iota((home, home), 0) < iota((home, home), 1))
        earlier = dot_nn(flags.astype(BF16), before)
        slot = jnp.sum(flags * earlier, axis=0, keepdims=True).astype(jnp.int32)
        tier = jnp.where(codes >= nt, 1, 0)
        place = (codes - nt * tier) * pair + tier * most + slot
        bmat[...] = flag(iota((nt * pair, home), 0) == place)
        gap = iota((MAXLEN, home), 1) - iota((MAXLEN, home), 0)
        offset = iota((MAXLEN, home), 0)
        for b in range(0, nb, 2):
            chosen = jnp.concatenate(
                [
                    jnp.where((gap == start[k]) & (offset < length[k]), 1.0, 0.0)
                    for k in (b, b + 1)
                ],
                axis=0,
            ).astype(BF16)
            smat[b * MAXLEN : (b + 2) * MAXLEN, :] = dot_nt(chosen, bmat[...]).astype(BF16)
        row = iota((home, WIN), 0)
        moved = jnp.zeros_like(row)
        for s in range(1, nb):
            moved = jnp.where(row >= in_off[s], s * WIN - in_off[s], moved)
        source = (row + moved)[:, :1]
        tmat[...] = flag(iota((home, nb * WIN), 1) == source)

    def x_to_y(c):
        for d in farthest_first(nt):
            x_copy(c, d, True).wait_recv()
        if c + ahead < chunks:
            x_start(c + ahead)
        xrecv[c][tab_id] = xsend[c][tab_id]
        width = widths[c]
        out = dot_nn(smat[...], xrecv[c][...].reshape(nt * pair, width))
        for b in range(nb):
            block = out[b * MAXLEN : (b + 1) * MAXLEN]
            if width > 128:
                block = jnp.concatenate([block[:, : width // 2], block[:, width // 2 :]], axis=0)
            else:
                block = jnp.concatenate([block, jnp.zeros((WIN - MAXLEN, width), F32)], axis=0)
            ysend[c][b] = block.astype(BF16)
        for d in farthest_first(nb):
            y_copy(c, d).start()
        yrecv[c][bal_id] = ysend[c][bal_id]

    def y_in(c):
        width = widths[c]
        for d in farthest_first(nb):
            y_copy(c, d, True).wait_recv()
        if width > 128:
            for s in range(nb):
                block = yrecv[c][s].astype(F32)
                block = jnp.concatenate([block[:MAXLEN], block[MAXLEN:]], axis=1)
                block = jnp.concatenate([block, jnp.zeros((WIN - MAXLEN, width), F32)], axis=0)
                spread[s * WIN : (s + 1) * WIN, :width] = block.astype(BF16)
            arrived = spread[:, :width]
        else:
            arrived = yrecv[c][...].reshape(nb * WIN, width)
        bal[:, firsts[c] : firsts[c] + width] = dot_nn(tmat[...], arrived).astype(BF16)

    def turn_out_grad():
        loads[3].wait()
        for b in range(nb):
            cols = 16 * nt
            turned = og[:, b * cols : (b + 1) * cols].T
            ogp[:, b * 16 : (b + 1) * 16, :] = turned.reshape(nt, 16, home)
        for x in range(nx):
            o_copy(x).start()

    def mask_scale(in_off):
        query, key = iota((TILE, 2 * TILE), 0), iota((TILE, 2 * TILE), 1)
        for i in range(tiles):
            at = query + i * TILE
            source = key + (i - 1) * TILE
            first = jnp.zeros_like(at)
            for s in range(1, nb):
                first = jnp.where(in_off[s] <= at, in_off[s], first)
            scale[i] = jnp.where((source <= at) & (source >= first), 0.5 * HEAD**-0.5, 0.0)

    step = 1024
    early = firsts[-2]

    def project_early():
        loads[4].wait()

        @pl.loop(0, 4 * model // step)
        def _(n):
            cols = pl.ds(pl.multiple_of(n * step, step), step)
            acc[:, cols] = dot_nn(bal[:, :early], w[:early, cols])

    def project_late():
        @pl.loop(0, 4 * model // step)
        def _(n):
            cols = pl.ds(pl.multiple_of(n * step, step), step)
            half = 0.5 * (acc[:, cols] + dot_nn(bal[:, early:], w[early:, cols]))
            prj[:, cols] = (half + half * jnp.tanh(half)).astype(BF16)

    def attend(i):
        rows = slice(i * TILE, (i + 1) * TILE)
        low = max(0, i - 1) * TILE
        keys = slice(low, (i + 1) * TILE)
        lanes = slice(2 * TILE - (i + 1) * TILE + low, 2 * TILE)

        @pl.loop(0, heads // 8)
        def _(some):
            def cols(part, k):
                at = part * model + (some * 8 + k) * HEAD
                return pl.ds(pl.multiple_of(at, HEAD), HEAD)

            scores = [dot_nt(prj[rows, cols(2, k)], prj[keys, cols(3, k)]) for k in range(8)]
            halves = [part * scale[i, :, lanes] for part in scores]
            weights = [(half + half * jnp.tanh(half)).astype(BF16) for half in halves]
            for k in range(8):
                asum[rows, cols(0, k)] = dot_nn(weights[k], prj[keys, cols(1, k)])

    def gate(i):
        rows = slice(i * TILE, (i + 1) * TILE)
        att[rows, :] = (normalize(asum[rows, :]) * prj[rows, :model].astype(F32)).astype(BF16)

    def partial_own(g):
        for x in range(nx):
            gown[g][x] = dot_nn(ogp[2 * x + core], att[:, columns(g)])

    def partial(g, x):
        if g < len(gown):
            own = gown[g][x]
        else:
            own = dot_nn(ogp[2 * x + core], att[:, columns(g)])
        return own + dot_nn(ogr[x], attr[:, columns(g)])

    def columns(g):
        return slice(gfirsts[g], gfirsts[g] + groups[g][1])

    def grad_start(g):
        axes, width, _ = groups[g]
        if axes == "xy":
            for d in farthest_first(nx) + [0]:
                x = lax.rem(x_id + d, nx)
                first_out[g][x] = partial(g, x).astype(BF16)
                if d:
                    first_copy(g, d).start()
        else:
            for x in range(nx):
                part = partial(g, x).astype(BF16)
                first_out[g][:, x * 16 : (x + 1) * 16, :] = part.reshape(nb, 16, width)
            for d in farthest_first(nb):
                first_copy(g, d).start()

    def gather(axis, copy, g, own, others):
        _, me, count = over(axis)
        total = own[g][me].astype(F32)
        for d in farthest_first(count)[::-1]:
            copy(g, d, True).wait_recv()
            total = total + others[g][lax.rem(me + d, count)].astype(F32)
        return total.astype(BF16)

    def grad_turn(g):
        axes, width, _ = groups[g]
        total = gather(axes[0], first_copy, g, first_out, first_in)
        _, _, count = over(axes[1])
        next_out[g][...] = total.reshape(count, 16, width)
        for d in farthest_first(count):
            next_copy(g, d).start()

    def grad_end(g):
        axes, width, whole = groups[g]
        total = gather(axes[1], next_copy, g, next_out, next_in)
        if whole:
            k = direct.index(g)
            whole_out[k][...] = total
            for d in farthest_first(nr):
                whole_copy(k, d).start()
            whole_in[k][rep_id] = total
        for j in range(nz):
            if owned[j][0] == g:
                at = owned[j][1] * TILE
                zs[j] = total[:, at : at + TILE]

                @pl.when(rep_id != j)
                def _():
                    z_copy(j).start()

    def grad_spread():
        @pl.when(rep_id < nz)
        def _():
            total = zs[rep_id].astype(F32)
            for d in range(1, nr):
                p = lax.rem(rep_id + d, nr)
                z_arrive(p).wait_recv()
                total = total + zr[p].astype(F32)
            zo[...] = total.astype(BF16)
            for d in farthest_first(nr):
                g_copy(d).start()
            zg[rep_id] = total.astype(BF16)

        for j in range(nz):

            @pl.when(rep_id != j)
            def _():
                g_arrive(j).wait_recv()

            at = gfirsts[owned[j][0]] + owned[j][1] * TILE
            grad_ref[:, at : at + TILE] = zg[j]
        for k, g in enumerate(direct):
            for d in range(1, nr):
                whole_copy(k, d, True).wait_recv()
            total = whole_in[k][0].astype(F32)
            for r in range(1, nr):
                total = total + whole_in[k][r].astype(F32)
            grad_ref[:, columns(g)] = total.astype(BF16)

    def all_sent():
        for c in range(chunks):
            for d in range(1, nt):
                x_copy(c, d).wait_send()
            for d in range(1, nb):
                y_copy(c, d).wait_send()
        for x in range(nx):
            o_copy(x).wait_send()
        for i in range(tiles):
            a_copy(i).wait_send()
        for g in range(gcount):
            for copy, axis in zip((first_copy, next_copy), groups[g][0]):
                for d in range(1, over(axis)[2]):
                    copy(g, d).wait_send()
        for k in range(len(direct)):
            for d in range(1, nr):
                whole_copy(k, d).wait_send()
        for j in range(nz):

            @pl.when(rep_id != j)
            def _():
                z_copy(j).wait_send()

        @pl.when(rep_id < nz)
        def _():
            for d in range(1, nr):
                g_copy(d).wait_send()

    load_and_greet()
    normalize_rows()
    greeted()
    hop_signal(0)
    for c in range(min(ahead, chunks)):
        x_start(c)
    start, length, in_off = history_bounds()
    placements(start, length, in_off)
    for c in range(chunks):
        x_to_y(c)
    turn_out_grad()
    mask_scale(in_off)
    for c in range(chunks - 1):
        y_in(c)
        if c < hops:
            hop_wait(c)
            if c + 1 < hops:
                hop_signal(c + 1)
        if c == chunks - 3:
            project_early()
    y_in(chunks - 1)
    project_late()
    for i in range(tiles):
        attend(i)
        gate(i)
        a_copy(i).start()
    att_copy.start()
    for g in range(len(gown)):
        partial_own(g)
    for x in range(nx):
        o_copy(x).wait_recv()
    for i in range(tiles):
        a_copy(i).wait_recv()
    for g in range(gcount):
        grad_start(g)
    for k in range(chunks - 1, hops):
        hop_wait(k)
        if k + 1 < hops:
            hop_signal(k + 1)
    for g in range(gcount):
        grad_turn(g)
    for g in range(gcount):
        grad_end(g)
    grad_spread()
    all_sent()
    att_copy.wait()


def hand_over(parts, att_in, grad_in, att_out, grad_out, att, grad, in_sem, out_sem):
    rows = att.shape[0] // parts
    views = [pl.ds(i * rows, rows) for i in range(parts)]
    steps = [(grad_in, grad, grad_out)]
    steps += [(att_in.at[view], att.at[view], att_out.at[view]) for view in views]
    fetches, stores = [], []
    for i, (source, held, target) in enumerate(steps):
        fetches.append(pltpu.make_async_copy(source, held, in_sem.at[i]))
        stores.append(pltpu.make_async_copy(held, target, out_sem.at[i]))
    for fetch in fetches:
        fetch.start()
    for fetch, store in zip(fetches, stores):
        fetch.wait()
        store.start()
    for store in stores:
        store.wait()


def on_device(sizes, hot_rows, cold_rows, row_source, lengths, destination, proj_weight, out_grad):
    nr, nb, nt = sizes
    home, model = out_grad.shape
    most = hot_rows.shape[0] // nt
    widths = (128, 256, 256, 256, 128)
    ahead = 2
    groups = (
        ("xy", 256, False), ("yx", 256, False), ("xy", 256, True), ("yx", 128, True),
        ("xy", 128, True),
    )
    chunks, gcount = len(widths), len(groups)
    nx, pair = nt // 2, 2 * most
    nz = sum(width // TILE for _, width, whole in groups if not whole)
    wholes = [width for _, width, whole in groups if whole]
    vmem = pltpu.VMEM
    dma = pltpu.SemaphoreType.DMA

    def y_block(width):
        return (2 * MAXLEN, width // 2) if width > 128 else (WIN, width)

    x_parts = [vmem((nt, pair, width), BF16) for width in widths]
    y_parts = [vmem((nb, *y_block(width)), BF16) for width in widths]
    def shares(axis, rows):
        return (nx, rows // nx) if axis == "x" else (nb, rows // nb)

    firsts = [vmem((*shares(axes[0], nx * nb * 16), width), BF16) for axes, width, _ in groups]
    nexts = [vmem((nx if axes[1] == "x" else nb, 16, width), BF16) for axes, width, _ in groups]
    scratch = [
        x_parts,
        x_parts,
        y_parts,
        y_parts,
        firsts,
        firsts,
        nexts,
        nexts,
        [vmem((16, width), BF16) for width in wholes],
        [vmem((nr, 16, width), BF16) for width in wholes],
        [vmem((nx, nb * 16, width), F32) for _, width, _ in groups[:2]],
        vmem((1, home), jnp.int32),
        pltpu.SMEM(lengths.shape, jnp.int32),
        pltpu.SMEM(destination.shape, jnp.int32),
        vmem(hot_rows.shape, F32),
        vmem(cold_rows.shape, BF16),
        vmem(proj_weight.shape, BF16),
        vmem(out_grad.shape, BF16),
        vmem((nt, nb * 16, home), BF16),
        vmem((nx, nb * 16, home), BF16),
        vmem((nt * pair, home), BF16),
        vmem((nb * MAXLEN, nt * pair), BF16),
        vmem((nb * WIN, max(widths)), BF16),
        vmem((home, nb * WIN), BF16),
        vmem((home, model), BF16),
        vmem((home, 4 * model), F32),
        vmem((home, 4 * model), BF16),
        vmem((home // TILE, TILE, 2 * TILE), F32),
        vmem((home, model), F32),
        vmem((home, model), BF16),
        vmem((home, model), BF16),
        vmem((nz, 16, TILE), BF16),
        vmem((nr, 16, TILE), BF16),
        vmem((16, TILE), BF16),
        vmem((nz, 16, TILE), BF16),
        dma((6,)),
        dma((2, nx)),
        dma((chunks, nt)),
        dma((chunks, nt)),
        dma((chunks, nb)),
        dma((chunks, nb)),
        dma((nx,)),
        dma((nx,)),
        dma((home // TILE,)),
        dma((home // TILE,)),
        dma((gcount, max(nx, nb))),
        dma((gcount, max(nx, nb))),
        dma((gcount, max(nx, nb))),
        dma((gcount, max(nx, nb))),
        dma((len(wholes), nr)),
        dma((len(wholes), nr)),
        dma((nz,)),
        dma((nr,)),
        dma((nr,)),
        dma((nz,)),
        pltpu.SemaphoreType.REGULAR((nr // 2 - 1, 2)),
    ]
    hbm = pl.BlockSpec(memory_space=pl.ANY)
    att, grad = pl.pallas_call(
        functools.partial(layer_kernel, nr, nb, nt, most, widths, ahead, groups),
        out_shape=(
            jax.ShapeDtypeStruct((home, model), BF16),
            jax.ShapeDtypeStruct((model // (nb * nt), model), BF16),
        ),
        in_specs=[hbm] * 7,
        out_specs=(hbm, pl.BlockSpec(memory_space=pltpu.VMEM)),
        scratch_shapes=scratch,
        compiler_params=pltpu.CompilerParams(
            collective_id=0, has_side_effects=True, vmem_limit_bytes=58 * 1024 * 1024
        ),
    )(
        hot_rows,
        cold_rows,
        row_source.reshape(1, home),
        lengths,
        destination,
        proj_weight,
        out_grad,
    )
    parts = 4
    return pl.pallas_call(
        functools.partial(hand_over, parts),
        out_shape=(
            jax.ShapeDtypeStruct(att.shape, att.dtype),
            jax.ShapeDtypeStruct(grad.shape, grad.dtype),
        ),
        in_specs=[hbm, hbm],
        out_specs=(hbm, hbm),
        scratch_shapes=[
            vmem(att.shape, att.dtype),
            vmem(grad.shape, grad.dtype),
            dma((parts + 1,)),
            dma((parts + 1,)),
        ],
    )(att, grad)


def solution(mesh):
    sizes = tuple(mesh.shape[axis] for axis in ("rep", "bal", "tab"))
    in_specs = (
        P(("rep", "bal", "tab"), None),
        P(("rep", "bal", "tab"), None),
        P(("rep", "bal", "tab"), None),
        P("rep", None, "tab", None),
        P("rep", None, "tab", None),
        P(),
        P(("rep", "bal", "tab"), None),
    )
    out_specs = (P(("rep", "bal", "tab"), None), P(("bal", "tab"), None))
    return jax.shard_map(
        functools.partial(on_device, sizes),
        mesh=mesh,
        in_specs=in_specs,
        out_specs=out_specs,
        check_vma=False,
    )
```
